256 devices in a mesh: wide: 64 (over z, y, core), narrow: 4 (over x).
Axes of the slice: x: 4, y: 4, z: 8, core: 2. Of those that a mesh axis runs over, the one named last changes fastest.
Arguments:
- tokens: bfloat16 [32768, 1024], P('wide'), may hold values from -1.5 to 1.5
- w_qk1: bfloat16 [1024, 1024], P(None, 'narrow')
- w_value1: bfloat16 [1024, 1024], P(None, 'narrow'), may hold values from -0.1875 to 0.1875
- w_out1: bfloat16 [1024, 1024], P('narrow'), may hold values from -0.1875 to 0.1875
- w_qk2: bfloat16 [1024, 1024], P(None, 'narrow')
- w_value2: bfloat16 [1024, 1024], P(None, 'narrow'), may hold values from -0.1875 to 0.1875
- w_out2: bfloat16 [1024, 1024], P('narrow'), may hold values from -0.5 to 0.5
- cluster_ids: int32 [8, 32768], P('narrow', 'wide'), may hold values from 0 to 31, as said below
Outputs:
- layer_out: float32 [32768, 1024], P('wide', 'narrow')
The draws below stay inside these ranges and needn't reach their ends.
Inputs may be any that keep to these rules, and one draw needn't show every extreme that they name: `cluster_ids`: within the 512 tokens of one index of wide, for each head, a quarter of the clusters hold 32 tokens each, half hold 12 and a quarter hold 8; which clusters are which is the same in every such block of one head.
All inputs are finite; a program needn't handle non-finite values.
Results may differ from the reference program's by a relative error of at most 0.022.
Values may be sent and summed in bfloat16 or wider, within the bound.
No kernel may reach another device: no remote copies, remote signals or barrier semaphores. Data moves between devices by JAX's collectives and lax.ppermute only.
A program may use at most 64 MiB of HBM per device.

```python
import math
import jax
import jax.numpy as jnp
from jax import lax

D = 1024
HEADS = 8
HEAD_DIM = 128
WINDOW = 256
TOK_DEV = 512
SEQ = 32768
NCLUS = 32
CAP = 32
N_WIDE = 64
N_NARROW = 4


def scaled_normal(key, factor):
    values = jax.random.normal(key, (D, D), jnp.float32) * (factor / math.sqrt(D))
    return values.astype(jnp.bfloat16)


def draw_w_qk1(key, part):
    key = jax.random.fold_in(key, 11)
    return scaled_normal(key, 0.5)


def draw_w_qk2(key, part):
    key = jax.random.fold_in(key, 13)
    return scaled_normal(key, 0.5)


def draw_cluster_ids(key, part):
    key = jax.random.fold_in(key, 21)
    blocks = SEQ // TOK_DEV
    quarter = NCLUS // 4
    ranks = jnp.arange(NCLUS, dtype=jnp.int32)
    quota = jnp.where(ranks < quarter, CAP, jnp.where(ranks < 3 * quarter, 3 * CAP // 8, CAP // 4))
    ends = jnp.cumsum(quota)
    places = jnp.arange(TOK_DEV, dtype=jnp.int32)
    rank_of_place = jnp.sum((ends[:, None] <= places[None, :]).astype(jnp.int32), axis=0)

    def one_head(head_key):
        order_key, block_key = jax.random.split(head_key)
        order = jax.random.permutation(order_key, NCLUS)
        labels = order[rank_of_place]
        shuffles = jax.vmap(lambda item: jax.random.permutation(item, TOK_DEV))(jax.random.split(block_key, blocks))
        return labels[shuffles].reshape(SEQ)
    return jax.vmap(one_head)(jax.random.split(key, HEADS)).astype(jnp.int32)


def steps_of(own_key, shape, shards, low, top_value):
    factor_of, own = 1.0, jax.random.fold_in(own_key, 6)
    for dim, shards_of in shards:
        heights = jnp.exp(jax.random.uniform(jax.random.fold_in(own, dim), (shards_of,), jnp.float32, low / len(shards), top_value / len(shards)))
        factor_of = factor_of * jnp.repeat(heights, shape[dim] // shards_of).reshape([-1 if axis == dim else 1 for axis in range(len(shape))])
    return factor_of


def scatter_about(own_key, dims, spread, most, cuts=(), kind=jnp.bfloat16):
    result = jax.random.normal(own_key, dims, jnp.float32) * spread
    if len(cuts) > 0:
        result = steps_of(own_key, dims, cuts, -0.22, 0.18) * result
    return jnp.clip(result, min=-most, max=most).astype(kind)


def setup_inputs(seed: int = 0) -> dict:
    splits = jax.random.split(jax.random.key(seed), 9)
    tokens = scatter_about(splits[0], (SEQ, D), 0.25, 1.5, ((0, 64),))
    w_qk1 = draw_w_qk1(jax.random.fold_in(splits[8], 71), 0)
    w_value1 = scatter_about(splits[2], (D, D), D ** -0.5, 0.1875, ((1, 4),))
    w_out1 = scatter_about(splits[3], (D, D), D ** -0.5, 0.1875, ((0, 4),))
    w_qk2 = draw_w_qk2(jax.random.fold_in(splits[8], 71), 0)
    w_value2 = scatter_about(splits[5], (D, D), D ** -0.5, 0.1875, ((1, 4),))
    w_out2 = scatter_about(splits[6], (D, D), HEAD_DIM ** -0.5, 0.5, ((0, 4),))
    cluster_ids = draw_cluster_ids(jax.random.fold_in(splits[8], 71), 0)
    return dict(tokens=tokens, w_qk1=w_qk1, w_value1=w_value1, w_out1=w_out1, w_qk2=w_qk2, w_value2=w_value2, w_out2=w_out2, cluster_ids=cluster_ids)


EPS = 1e-06

def rms_round(rows):
    values = rows.astype(jnp.float32)
    factor = lax.rsqrt(lax.optimization_barrier(jnp.mean(values * values, axis=-1, keepdims=True)) + EPS)
    return (values * factor).astype(jnp.bfloat16)

def project(normed, weight):
    return jnp.dot(normed, weight, preferred_element_type=jnp.float32).astype(jnp.bfloat16)

def window_attention(query, keys, values):
    length = query.shape[0]
    block = min(512, length)
    heads = query.shape[1] // HEAD_DIM
    factor = 1.0 / math.sqrt(HEAD_DIM)

    def one_block(start):
        q = lax.dynamic_slice_in_dim(query, start, block, 0).reshape(block, heads, HEAD_DIM).astype(jnp.float32)
        k = lax.dynamic_slice_in_dim(keys, start, block + WINDOW, 0).reshape(block + WINDOW, heads, HEAD_DIM).astype(jnp.float32)
        v = lax.dynamic_slice_in_dim(values, start, block + WINDOW, 0).reshape(block + WINDOW, heads, HEAD_DIM).astype(jnp.float32)
        scores = jnp.einsum('qhd,khd->hqk', q, k, precision=lax.Precision.HIGHEST) * factor
        qpos = start + jnp.arange(block, dtype=jnp.int32)
        kpos = start - WINDOW + jnp.arange(block + WINDOW, dtype=jnp.int32)
        gap = qpos[:, None] - kpos[None, :]
        keep = (gap > 0) & (gap < WINDOW) & (kpos[None, :] >= 0) | (gap == 0) & (qpos[:, None] == 0)
        scores = jnp.where(keep[None], scores, -1e+30)
        top = lax.optimization_barrier(jnp.max(scores, axis=-1, keepdims=True))
        weights = jnp.exp(scores - top)
        totals = lax.optimization_barrier(jnp.sum(weights, axis=-1))
        rounded = weights.astype(jnp.bfloat16).astype(jnp.float32)
        mixed = jnp.einsum('hqk,khd->qhd', rounded, v, precision=lax.Precision.HIGHEST)
        mixed = mixed / jnp.transpose(totals)[:, :, None]
        return mixed.reshape(block, heads * HEAD_DIM).astype(jnp.bfloat16)
    starts = jnp.arange(length // block, dtype=jnp.int32) * block
    return lax.map(one_block, starts).reshape(length, heads * HEAD_DIM)

def grouped_sum(mixed, weight):
    step = D // N_NARROW
    total = jnp.zeros((mixed.shape[0], D), jnp.float32)
    for group in range(N_NARROW):
        term = jnp.dot(mixed[:, group * step:(group + 1) * step], weight[group * step:(group + 1) * step], preferred_element_type=jnp.float32)
        total = total + term.astype(jnp.bfloat16).astype(jnp.float32)
    return total

def cluster_attention(shared, values, labels):
    most = N_WIDE * CAP
    block = min(512, most)
    factor = 1.0 / math.sqrt(HEAD_DIM)
    match = labels[:, None] == jnp.arange(NCLUS, dtype=jnp.int32)[None, :]
    running = jnp.cumsum(match.astype(jnp.int32), axis=0)
    rank = (lax.optimization_barrier(jnp.sum(jnp.where(match, running, 0), axis=1)) - 1).astype(jnp.int32)
    table = jnp.full((NCLUS, most), SEQ, jnp.int32).at[labels, rank].set(jnp.arange(SEQ, dtype=jnp.int32))
    order = jnp.arange(most, dtype=jnp.int32)

    def one_cluster(members):
        live = members < SEQ
        safe = jnp.minimum(members, SEQ - 1)
        kc = shared[safe].astype(jnp.float32)
        vc = values[safe].astype(jnp.float32)

        def one_block(start):
            q = lax.dynamic_slice_in_dim(kc, start, block, 0)
            scores = jnp.dot(q, kc.T, precision=lax.Precision.HIGHEST) * factor
            rows_here = start + jnp.arange(block, dtype=jnp.int32)
            earlier = order[None, :] < rows_here[:, None]
            alone = (order[None, :] == rows_here[:, None]) & (rows_here[:, None] == 0)
            keep = (earlier | alone) & live[None, :]
            scores = jnp.where(keep, scores, -1e+30)
            top = lax.optimization_barrier(jnp.max(scores, axis=-1, keepdims=True))
            weights = jnp.exp(scores - top)
            totals = lax.optimization_barrier(jnp.sum(weights, axis=-1))
            rounded = weights.astype(jnp.bfloat16).astype(jnp.float32)
            mixed = jnp.dot(rounded, vc, precision=lax.Precision.HIGHEST) / totals[:, None]
            return mixed.astype(jnp.bfloat16)
        starts = jnp.arange(most // block, dtype=jnp.int32) * block
        return lax.map(one_block, starts).reshape(most, HEAD_DIM)
    results = lax.map(one_cluster, table)
    placed = jnp.zeros((SEQ, HEAD_DIM), jnp.bfloat16)
    return placed.at[table.reshape(-1)].set(results.reshape(-1, HEAD_DIM), mode='drop')

def reference(tokens, w_qk1, w_value1, w_out1, w_qk2, w_value2, w_out2, cluster_ids):
    normed = rms_round(tokens)
    qk1 = project(normed, w_qk1)
    value1 = project(normed, w_value1)
    padding = jnp.zeros((WINDOW, D), jnp.bfloat16)
    attended1 = window_attention(qk1, jnp.concatenate([padding, qk1], axis=0), jnp.concatenate([padding, value1], axis=0))
    hidden = (tokens.astype(jnp.float32) + grouped_sum(attended1, w_out1)).astype(jnp.bfloat16)
    normed2 = rms_round(hidden)
    qk2 = project(normed2, w_qk2)
    value2 = project(normed2, w_value2)
    outputs = []
    for head in range(HEADS):
        cols = slice(head * HEAD_DIM, (head + 1) * HEAD_DIM)
        outputs.append(cluster_attention(qk2[:, cols], value2[:, cols], cluster_ids[head]))
    attended2 = jnp.concatenate(outputs, axis=1)
    return hidden.astype(jnp.float32) + grouped_sum(attended2, w_out2)
```

```python
import functools
import math

import jax
import jax.numpy as jnp
from jax import lax
from jax.experimental import pallas as pl
from jax.experimental.pallas import tpu as pltpu
from jax.sharding import PartitionSpec as P

HEAD_DIM = 128
WINDOW = 256
EPS = 1e-06
MASKED = -1e30
EXP2_FACTOR = math.log2(math.e) / math.sqrt(HEAD_DIM)
CLUSTERS = 32
SLOTS = 512
BF16 = jnp.bfloat16
F32 = jnp.float32


def call(body, outs, args, scratch=(), prefetch=0, flops=0, bytes_accessed=0):
    whole = [pl.BlockSpec(memory_space=pltpu.SMEM)] * prefetch + [
        pl.BlockSpec(memory_space=pltpu.VMEM)
    ] * (len(args) - prefetch)
    return pl.pallas_call(
        body,
        out_shape=outs,
        in_specs=whole,
        out_specs=jax.tree.map(lambda _: pl.BlockSpec(memory_space=pltpu.VMEM), outs),
        scratch_shapes=list(scratch),
        compiler_params=pltpu.CompilerParams(vmem_limit_bytes=40 * 2**20),
        cost_estimate=pl.CostEstimate(
            flops=flops, bytes_accessed=bytes_accessed, transcendentals=0
        ),
    )(*args)


def rms_round(values):
    factor = lax.rsqrt(jnp.mean(values * values, axis=-1, keepdims=True) + EPS)
    return (values * factor).astype(BF16)


def matmul(left, right):
    return jnp.dot(left, right, preferred_element_type=F32)


def scores_of(query, keys):
    return lax.dot_general(query, keys, (((1,), (1,)), ((), ())), preferred_element_type=F32)


def front_body(tokens_ref, w_qk_ref, w_value_ref, qk_ref, value_ref, tail_ref):
    normed = rms_round(tokens_ref[...].astype(F32))
    qk = matmul(normed, w_qk_ref[...]).astype(BF16)
    value = matmul(normed, w_value_ref[...]).astype(BF16)
    length = qk.shape[0]
    qk_ref[...] = qk
    value_ref[...] = value
    tail_ref[0] = qk[length - WINDOW :]
    tail_ref[1] = value[length - WINDOW :]


def window_body(first_ref, qk_ref, value_ref, before_ref, out_ref):
    tile = WINDOW
    row = lax.broadcasted_iota(jnp.int32, (tile, 2 * tile), 0)
    col = lax.broadcasted_iota(jnp.int32, (tile, 2 * tile), 1)
    band = (col > row) & (col < row + WINDOW)
    at_start = first_ref[0] == 0
    opening = (band & (col >= tile)) | ((row == 0) & (col == tile))
    first_band = (jnp.logical_not(at_start) & band) | (at_start & opening)
    length = qk_ref.shape[0]
    ones = jnp.ones((2 * tile, HEAD_DIM), BF16)
    for head in range(2):
        cols = slice(head * HEAD_DIM, (head + 1) * HEAD_DIM)
        for part in range(length // tile):
            query = qk_ref[part * tile : (part + 1) * tile, cols]
            if part == 0:
                keys = jnp.concatenate([before_ref[0, :, cols], query], axis=0)
                values = jnp.concatenate([before_ref[1, :, cols], value_ref[:tile, cols]], axis=0)
            else:
                keys = qk_ref[(part - 1) * tile : (part + 1) * tile, cols]
                values = value_ref[(part - 1) * tile : (part + 1) * tile, cols]
            scores = jnp.where(first_band if part == 0 else band, scores_of(query, keys), MASKED)
            top = jnp.max(scores, axis=-1, keepdims=True)
            weights = jnp.exp2((scores - top) * EXP2_FACTOR).astype(BF16)
            mixed = matmul(weights, jnp.concatenate([values, ones], axis=1))
            out_ref[head, part * tile : (part + 1) * tile] = (
                mixed[:, :HEAD_DIM] / mixed[:, HEAD_DIM:]
            ).astype(BF16)


def place_body(ids_ref, place_ref, place_col_ref):
    length = ids_ref.shape[1]
    earlier = (
        lax.broadcasted_iota(jnp.int32, (length, length), 0)
        < lax.broadcasted_iota(jnp.int32, (length, length), 1)
    ).astype(F32).astype(BF16)
    same = lax.broadcasted_iota(jnp.int32, (length, length), 0) == lax.broadcasted_iota(
        jnp.int32, (length, length), 1
    )
    lower = (
        lax.broadcasted_iota(jnp.int32, (CLUSTERS, CLUSTERS), 1)
        < lax.broadcasted_iota(jnp.int32, (CLUSTERS, CLUSTERS), 0)
    ).astype(F32).astype(BF16)
    for head in range(2):
        ids = ids_ref[head : head + 1, :]
        match = (
            lax.broadcasted_iota(jnp.int32, (CLUSTERS, length), 0) == ids
        ).astype(F32)
        rank = matmul(match.astype(BF16), earlier)
        count = jnp.sum(match, axis=1, keepdims=True)
        count = jnp.broadcast_to(count, (CLUSTERS, 128))
        large = count > 20.0
        small = count < 10.0
        middle = jnp.logical_not(large | small)
        one = lambda kind: matmul(lower, kind.astype(F32).astype(BF16))
        at_large = one(large) * 32.0
        nth = one(middle)
        pair = jnp.floor(nth * 0.5)
        at_middle = 256.0 + pair * 32.0 + (nth - 2.0 * pair) * 12.0
        at_small = 256.0 + one(small) * 32.0 + 24.0
        base = jnp.where(large, at_large, jnp.where(small, at_small, at_middle))[:, :1]
        place = jnp.sum(match * (rank + base), axis=0, keepdims=True)
        place_ref[head : head + 1, :] = place.astype(jnp.int32)
        column = jnp.sum(jnp.where(same, place, 0.0), axis=1, keepdims=True)
        place_col_ref[:, head : head + 1] = column.astype(jnp.int32)


def middle_body(
    core_ref,
    tokens_ref,
    own_ref,
    left_ref,
    right_ref,
    far0_ref,
    far1_ref,
    w_own_ref,
    w_left_ref,
    w_right_ref,
    w_far_ref,
    x_own_ref,
    x_left_ref,
    x_right_ref,
    x_far_ref,
    w_qk_ref,
    w_value_ref,
    place_ref,
    hidden_ref,
    out_ref,
    far_ref,
):
    core = core_ref[0]
    far_ref[0] = far0_ref[...]
    far_ref[1] = far1_ref[...]
    left_side = []
    right_side = []
    for att, mine, other in (
        (own_ref, w_own_ref, x_own_ref),
        (left_ref, w_left_ref, x_left_ref),
        (right_ref, w_right_ref, x_right_ref),
        (far_ref, w_far_ref, x_far_ref),
    ):
        left_side += [att[core], att[1 - core]]
        right_side += [mine[...], other[...]]
    mixed = matmul(jnp.concatenate(left_side, axis=1), jnp.concatenate(right_side, axis=0))
    hidden = (tokens_ref[...].astype(F32) + mixed).astype(BF16)
    hidden_ref[...] = hidden
    normed = rms_round(hidden.astype(F32))
    qk = matmul(normed, w_qk_ref[...]).astype(BF16)
    value = matmul(normed, w_value_ref[...]).astype(BF16)
    length = qk.shape[0]
    for head in range(2):
        cols = slice(head * HEAD_DIM, (head + 1) * HEAD_DIM)
        spot = lax.broadcasted_iota(jnp.int32, (SLOTS, length), 0)
        pick = (spot == place_ref[head : head + 1, :]).astype(F32).astype(BF16)
        rows = jnp.concatenate([qk[:, cols], value[:, cols]], axis=1)
        out_ref[head] = matmul(pick, rows).astype(BF16)


def cluster_body(info_ref, mine_ref, other_ref, out_ref, keys_ref, values_ref, query_ref):
    core = info_ref[0]
    whole = info_ref[1] == 1
    rows = mine_ref.shape[0]
    lane = lax.broadcasted_iota(jnp.int32, (rows, HEAD_DIM), 1)
    row = lax.broadcasted_iota(jnp.int32, (rows, HEAD_DIM), 0) & 15

    def segment(which):
        slot = row + 16 * which
        found = jnp.where(slot >= 24, 2, jnp.where(slot >= 12, 1, 0))
        return jnp.where(whole, 0, found)

    seg_mine = segment(core)
    seg_other = segment(1 - core)
    query_ref[:, :HEAD_DIM] = mine_ref[:, :HEAD_DIM]
    query_ref[:, HEAD_DIM:] = jnp.where(lane == seg_mine, 0.0, MASKED).astype(BF16)
    for side, (source, seg) in enumerate(((mine_ref, seg_mine), (other_ref, seg_other))):
        keys_ref[side, :, :HEAD_DIM] = source[:, :HEAD_DIM]
        keys_ref[side, :, HEAD_DIM:] = jnp.where(lane == seg, 1.0, 0.0).astype(BF16)
        values_ref[side, :, :HEAD_DIM] = source[:, HEAD_DIM:]
        values_ref[side, :, HEAD_DIM:] = jnp.ones((rows, HEAD_DIM), BF16)
    tile = 256
    near_row = lax.broadcasted_iota(jnp.int32, (tile, tile), 0)
    near_col = lax.broadcasted_iota(jnp.int32, (tile, tile), 1)
    earlier = near_col < near_row
    block_row = near_row >> 4
    block_col = near_col >> 4
    earlier_other = block_col < block_row + core
    slot = (near_row & 15) + 16 * core
    opens = (slot == 0) | (jnp.logical_not(whole) & ((slot == 12) | (slot == 24)))
    alone = (near_row == near_col) & opens & (near_row < 16)
    for part in range(rows // tile):
        here = slice(part * tile, (part + 1) * tile)
        query = query_ref[here, :]
        keep = (earlier | alone) if part == 0 else earlier
        groups = []
        for side in range(2):
            if part > 0:
                past = slice(0, part * tile)
                groups.append((scores_of(query, keys_ref[side, past, :]), side, past))
            near = scores_of(query, keys_ref[side, here, :])
            near = jnp.where(keep if side == 0 else earlier_other, near, MASKED)
            groups.append((near, side, here))
        top = functools.reduce(
            jnp.maximum, [jnp.max(scores, axis=-1, keepdims=True) for scores, _, _ in groups]
        )
        mixed = jnp.zeros((tile, 2 * HEAD_DIM), F32)
        for scores, side, span in groups:
            weights = jnp.exp2((scores - top) * EXP2_FACTOR).astype(BF16)
            mixed += matmul(weights, values_ref[side, span, :])
        out_ref[here, :] = (mixed[:, :HEAD_DIM] / mixed[:, HEAD_DIM:]).astype(BF16)


def back_body(returned_ref, place_col_ref, out_ref):
    length = place_col_ref.shape[0]
    for head in range(2):
        spot = lax.broadcasted_iota(jnp.int32, (length, SLOTS), 1)
        pick = (spot == place_col_ref[:, head : head + 1]).astype(F32).astype(BF16)
        out_ref[head] = matmul(pick, returned_ref[head]).astype(BF16)


def last_body(
    own_ref, left_ref, right_ref, far0_ref, far1_ref, w_own_ref, w_left_ref, w_right_ref,
    w_far_ref, hidden_ref, out_ref,
):
    left_side = [
        own_ref[0], own_ref[1], left_ref[0], left_ref[1],
        right_ref[0], right_ref[1], far0_ref[...], far1_ref[...],
    ]
    right_side = [w_own_ref[...], w_left_ref[...], w_right_ref[...], w_far_ref[...]]
    mixed = matmul(jnp.concatenate(left_side, axis=1), jnp.concatenate(right_side, axis=0))
    out_ref[...] = hidden_ref[...].astype(F32) + mixed


def around(value, steps):
    count = lax.axis_size("narrow")
    return lax.ppermute(value, "narrow", [(i, (i + steps) % count) for i in range(count)])


def swap_cores(value):
    count = lax.axis_size("wide")
    return lax.ppermute(value, "wide", [(i, i ^ 1) for i in range(count)])


def gather_pair(value):
    left = around(value, 1)
    right = around(value, -1)
    far0 = around(left[0], 1)
    far1 = around(right[1], -1)
    return left, right, far0, far1


def shards(tokens, w_qk1, w_value1, w_out1, w_qk2, w_value2, w_out2, cluster_ids):
    length, width = tokens.shape
    shape = jax.ShapeDtypeStruct
    wide = lax.axis_index("wide")
    narrow = lax.axis_index("narrow")
    wide_count = lax.axis_size("wide")
    groups = lax.axis_size("narrow")
    core = wide % 2
    group_width = w_qk1.shape[1]

    half = lax.dynamic_slice_in_dim(w_out1, core * HEAD_DIM, HEAD_DIM, 0)
    half = half.reshape(2, HEAD_DIM // 2, width)
    w_left, w_right, w_far0, w_far1 = gather_pair(half)
    w_mine = [
        item.reshape(HEAD_DIM, width)
        for item in (half, w_left, w_right, jnp.stack([w_far0, w_far1]))
    ]

    qk1, value1, tails = call(
        front_body,
        (
            shape((length, group_width), BF16),
            shape((length, group_width), BF16),
            shape((2, WINDOW, group_width), BF16),
        ),
        (tokens, w_qk1, w_value1),
        flops=2 * length * width * group_width * 2,
        bytes_accessed=3 * 2**20,
    )
    before = lax.ppermute(tails, "wide", [(i, i + 1) for i in range(wide_count - 1)])
    place, place_col = call(
        place_body,
        (shape((2, length), jnp.int32), shape((length, 2), jnp.int32)),
        (cluster_ids,),
        flops=2**26,
        bytes_accessed=2**18,
    )
    attended1 = call(
        window_body,
        shape((2, length, HEAD_DIM), BF16),
        (wide.reshape(1), qk1, value1, before),
        prefetch=1,
        flops=2**28,
        bytes_accessed=2**20,
    )
    w_other = [swap_cores(item) for item in w_mine]
    left, right, far0, far1 = gather_pair(attended1)
    hidden, outgoing = call(
        middle_body,
        (shape((length, width), BF16), shape((2, SLOTS, 2 * HEAD_DIM), BF16)),
        (
            core.reshape(1), tokens, attended1, left, right, far0, far1,
            *w_mine, *w_other, w_qk2, w_value2, place,
        ),
        scratch=(pltpu.VMEM((2, length, HEAD_DIM), BF16),),
        prefetch=1,
        flops=2**31,
        bytes_accessed=2**23,
    )
    per_pair = 2 * SLOTS // wide_count
    arrived = lax.all_to_all(
        outgoing.reshape(wide_count, per_pair, 2 * HEAD_DIM), "wide", 0, 0, tiled=True
    ).reshape(2 * SLOTS, 2 * HEAD_DIM)
    other = swap_cores(arrived)
    info = jnp.stack([core, ((wide // 2) % 16 < 8).astype(jnp.int32)])
    rows = 2 * SLOTS
    answers = call(
        cluster_body,
        shape((rows, HEAD_DIM), BF16),
        (info, arrived, other),
        scratch=(
            pltpu.VMEM((2, rows, 2 * HEAD_DIM), BF16),
            pltpu.VMEM((2, rows, 2 * HEAD_DIM), BF16),
            pltpu.VMEM((rows, 2 * HEAD_DIM), BF16),
        ),
        prefetch=1,
        flops=2**30,
        bytes_accessed=2**21,
    )
    returned = lax.all_to_all(
        answers.reshape(wide_count, per_pair, HEAD_DIM), "wide", 0, 0, tiled=True
    ).reshape(2, SLOTS, HEAD_DIM)
    attended2 = call(
        back_body,
        shape((2, length, HEAD_DIM), BF16),
        (returned, place_col),
        flops=2**27,
        bytes_accessed=2**20,
    )
    left, right, far0, far1 = gather_pair(attended2)

    def columns_for(steps):
        target = (narrow + steps) % groups
        return lax.dynamic_slice_in_dim(w_out2, target * group_width, group_width, 1)

    w_own2 = columns_for(0)
    w_left2 = around(columns_for(1), 1)
    w_right2 = around(columns_for(-1), -1)
    w_far2 = around(columns_for(2), 2)
    hidden_own = lax.dynamic_slice_in_dim(hidden, narrow * group_width, group_width, 1)
    return call(
        last_body,
        shape((length, group_width), F32),
        (
            attended2, left, right, far0, far1, w_own2, w_left2, w_right2, w_far2, hidden_own,
        ),
        flops=2**29,
        bytes_accessed=2**21,
    )


def solution(mesh):
    placed = (
        P("wide", None),
        P(None, "narrow"),
        P(None, "narrow"),
        P("narrow", None),
        P(None, "narrow"),
        P(None, "narrow"),
        P("narrow", None),
        P("narrow", "wide"),
    )
    return jax.shard_map(
        shards, mesh=mesh, in_specs=placed, out_specs=P("wide", "narrow"), check_vma=False
    )
```

```python
import functools
import math

import jax
import jax.numpy as jnp
from jax import lax
from jax.experimental import pallas as pl
from jax.experimental.pallas import tpu as pltpu
from jax.sharding import PartitionSpec as P

HEAD_DIM = 128
WINDOW = 256
EPS = 1e-06
MASKED = -1e30
EXP2_FACTOR = math.log2(math.e) / math.sqrt(HEAD_DIM)
CLUSTERS = 32
SLOTS = 512
BF16 = jnp.bfloat16
F32 = jnp.float32


def call(
    body, outs, args, scratch=(), prefetch=0, flops=0, bytes_accessed=0, space=pltpu.VMEM,
    mib=20,
):
    whole = [pl.BlockSpec(memory_space=pltpu.SMEM)] * prefetch + [
        pl.BlockSpec(memory_space=space)
    ] * (len(args) - prefetch)
    return pl.pallas_call(
        body,
        out_shape=outs,
        in_specs=whole,
        out_specs=jax.tree.map(lambda _: pl.BlockSpec(memory_space=pltpu.VMEM), outs),
        scratch_shapes=list(scratch),
        compiler_params=pltpu.CompilerParams(vmem_limit_bytes=mib * 2**20),
        cost_estimate=pl.CostEstimate(
            flops=flops, bytes_accessed=bytes_accessed, transcendentals=0
        ),
    )(*args)


def rms_round(values):
    factor = lax.rsqrt(jnp.mean(values * values, axis=-1, keepdims=True) + EPS)
    return (values * factor).astype(BF16)


def matmul(left, right):
    return jnp.dot(left, right, preferred_element_type=F32)


def scores_of(query, keys):
    return lax.dot_general(query, keys, (((1,), (1,)), ((), ())), preferred_element_type=F32)


def front_body(
    tokens_any, w_qk_any, w_value_any, qk_ref, value_ref, tail_ref,
    tokens_ref, w_qk_ref, w_value_ref, sems,
):
    length = tokens_ref.shape[0]
    parts = 2
    step = length // parts
    spans = [slice(part * step, (part + 1) * step) for part in range(parts)]
    token_copies = [
        pltpu.make_async_copy(tokens_any.at[span], tokens_ref.at[span], sems.at[2 + part])
        for part, span in enumerate(spans)
    ]
    qk_copy = pltpu.make_async_copy(w_qk_any, w_qk_ref, sems.at[0])
    value_copy = pltpu.make_async_copy(w_value_any, w_value_ref, sems.at[1])
    for copy in (token_copies[0], qk_copy, value_copy, *token_copies[1:]):
        copy.start()
    for part, span in enumerate(spans):
        token_copies[part].wait()
        normed = rms_round(tokens_ref[span].astype(F32))
        if part == 0:
            qk_copy.wait()
        qk = matmul(normed, w_qk_ref[...]).astype(BF16)
        if part == 0:
            value_copy.wait()
        value = matmul(normed, w_value_ref[...]).astype(BF16)
        qk_ref[span] = qk
        value_ref[span] = value
        if part == parts - 1:
            tail_ref[0] = qk[step - WINDOW :]
            tail_ref[1] = value[step - WINDOW :]


def window_body(first_ref, qk_ref, value_ref, before_ref, out_ref):
    tile = WINDOW
    row = lax.broadcasted_iota(jnp.int32, (tile, 2 * tile), 0)
    col = lax.broadcasted_iota(jnp.int32, (tile, 2 * tile), 1)
    band = (col > row) & (col < row + WINDOW)
    at_start = first_ref[0] == 0
    opening = (band & (col >= tile)) | ((row == 0) & (col == tile))
    first_band = (jnp.logical_not(at_start) & band) | (at_start & opening)
    length = qk_ref.shape[0]
    ones = jnp.ones((2 * tile, HEAD_DIM), BF16)
    for head in range(2):
        cols = slice(head * HEAD_DIM, (head + 1) * HEAD_DIM)
        for part in range(length // tile):
            query = qk_ref[part * tile : (part + 1) * tile, cols]
            if part == 0:
                keys = jnp.concatenate([before_ref[0, :, cols], query], axis=0)
                values = jnp.concatenate([before_ref[1, :, cols], value_ref[:tile, cols]], axis=0)
            else:
                keys = qk_ref[(part - 1) * tile : (part + 1) * tile, cols]
                values = value_ref[(part - 1) * tile : (part + 1) * tile, cols]
            scores = jnp.where(first_band if part == 0 else band, scores_of(query, keys), MASKED)
            top = jnp.max(scores, axis=-1, keepdims=True)
            weights = jnp.exp2((scores - top) * EXP2_FACTOR).astype(BF16)
            mixed = matmul(weights, jnp.concatenate([values, ones], axis=1))
            out_ref[part * tile : (part + 1) * tile, cols] = (
                mixed[:, :HEAD_DIM] / mixed[:, HEAD_DIM:]
            ).astype(BF16)


def place_body(
    ids_any, w_out_any, w_qk_any, w_value_any,
    place_ref, place_col_ref, w_out_ref, w_qk_ref, w_value_ref, ids_ref, sems,
):
    copies = [
        pltpu.make_async_copy(source, target, sems.at[index])
        for index, (source, target) in enumerate(
            (
                (ids_any, ids_ref), (w_out_any, w_out_ref),
                (w_qk_any, w_qk_ref), (w_value_any, w_value_ref),
            )
        )
    ]
    for copy in copies:
        copy.start()
    copies[0].wait()
    length = ids_ref.shape[1]
    earlier = (
        lax.broadcasted_iota(jnp.int32, (length, length), 0)
        < lax.broadcasted_iota(jnp.int32, (length, length), 1)
    ).astype(F32).astype(BF16)
    same = lax.broadcasted_iota(jnp.int32, (length, length), 0) == lax.broadcasted_iota(
        jnp.int32, (length, length), 1
    )
    lower = (
        lax.broadcasted_iota(jnp.int32, (CLUSTERS, CLUSTERS), 1)
        < lax.broadcasted_iota(jnp.int32, (CLUSTERS, CLUSTERS), 0)
    ).astype(F32).astype(BF16)
    for head in range(2):
        ids = ids_ref[head : head + 1, :]
        match = (
            lax.broadcasted_iota(jnp.int32, (CLUSTERS, length), 0) == ids
        ).astype(F32)
        rank = matmul(match.astype(BF16), earlier)
        count = jnp.sum(match, axis=1, keepdims=True)
        count = jnp.broadcast_to(count, (CLUSTERS, 128))
        large = count > 20.0
        small = count < 10.0
        middle = jnp.logical_not(large | small)
        one = lambda kind: matmul(lower, kind.astype(F32).astype(BF16))
        at_large = one(large) * 32.0
        nth = one(middle)
        pair = jnp.floor(nth * 0.5)
        at_middle = 256.0 + pair * 32.0 + (nth - 2.0 * pair) * 12.0
        at_small = 256.0 + one(small) * 32.0 + 24.0
        base = jnp.where(large, at_large, jnp.where(small, at_small, at_middle))[:, :1]
        place = jnp.sum(match * (rank + base), axis=0, keepdims=True)
        place_ref[head : head + 1, :] = place.astype(jnp.int32)
        column = jnp.sum(jnp.where(same, place, 0.0), axis=1, keepdims=True)
        place_col_ref[:, head : head + 1] = column.astype(jnp.int32)
    for copy in copies[1:]:
        copy.wait()


def middle_body(
    core_ref,
    tokens_ref,
    own_ref,
    first_ref,
    second_ref,
    far_ref,
    w_own_ref,
    w_first_ref,
    w_second_ref,
    w_far_mine_ref,
    w_far_other_ref,
    w_qk_ref,
    w_value_ref,
    place_ref,
    hidden_ref,
    out_ref,
):
    even = core_ref[0] == 0
    far_mine = w_far_mine_ref[...]
    far_other = w_far_other_ref[...]
    left_side = [own_ref[...], first_ref[...], second_ref[...], far_ref[...]]
    right_side = [
        w_own_ref[...],
        w_first_ref[...],
        w_second_ref[...],
        jnp.where(even, far_mine, far_other),
        jnp.where(even, far_other, far_mine),
    ]
    mixed = matmul(jnp.concatenate(left_side, axis=1), jnp.concatenate(right_side, axis=0))
    hidden = (tokens_ref[...].astype(F32) + mixed).astype(BF16)
    hidden_ref[...] = hidden
    normed = rms_round(hidden.astype(F32))
    qk = matmul(normed, w_qk_ref[...]).astype(BF16)
    value = matmul(normed, w_value_ref[...]).astype(BF16)
    length = qk.shape[0]
    for head in range(2):
        cols = slice(head * HEAD_DIM, (head + 1) * HEAD_DIM)
        spot = lax.broadcasted_iota(jnp.int32, (SLOTS, length), 0)
        pick = (spot == place_ref[head : head + 1, :]).astype(F32).astype(BF16)
        rows = jnp.concatenate([qk[:, cols], value[:, cols]], axis=1)
        out_ref[head] = matmul(pick, rows).astype(BF16)


def cluster_body(info_ref, mine_ref, other_ref, out_ref, keys_ref, values_ref, query_ref):
    core = info_ref[0]
    whole = info_ref[1] == 1
    rows = mine_ref.shape[0]
    lane = lax.broadcasted_iota(jnp.int32, (rows, HEAD_DIM), 1)
    row = lax.broadcasted_iota(jnp.int32, (rows, HEAD_DIM), 0) & 15

    def segment(which):
        slot = row + 16 * which
        found = jnp.where(slot >= 24, 2, jnp.where(slot >= 12, 1, 0))
        return jnp.where(whole, 0, found)

    seg_mine = segment(core)
    seg_other = segment(1 - core)
    query_ref[:, :HEAD_DIM] = mine_ref[:, :HEAD_DIM]
    query_ref[:, HEAD_DIM:] = jnp.where(lane == seg_mine, 0.0, MASKED).astype(BF16)
    for side, (source, seg) in enumerate(((mine_ref, seg_mine), (other_ref, seg_other))):
        keys_ref[side, :, :HEAD_DIM] = source[:, :HEAD_DIM]
        keys_ref[side, :, HEAD_DIM:] = jnp.where(lane == seg, 1.0, 0.0).astype(BF16)
        values_ref[side, :, :HEAD_DIM] = source[:, HEAD_DIM:]
        values_ref[side, :, HEAD_DIM:] = jnp.ones((rows, HEAD_DIM), BF16)
    tile = 256
    near_row = lax.broadcasted_iota(jnp.int32, (tile, tile), 0)
    near_col = lax.broadcasted_iota(jnp.int32, (tile, tile), 1)
    earlier = near_col < near_row
    block_row = near_row >> 4
    block_col = near_col >> 4
    earlier_other = block_col < block_row + core
    slot = (near_row & 15) + 16 * core
    opens = (slot == 0) | (jnp.logical_not(whole) & ((slot == 12) | (slot == 24)))
    alone = (near_row == near_col) & opens & (near_row < 16)
    for part in range(rows // tile):
        here = slice(part * tile, (part + 1) * tile)
        query = query_ref[here, :]
        keep = (earlier | alone) if part == 0 else earlier
        groups = []
        for side in range(2):
            if part > 0:
                past = slice(0, part * tile)
                groups.append((scores_of(query, keys_ref[side, past, :]), side, past))
            near = scores_of(query, keys_ref[side, here, :])
            near = jnp.where(keep if side == 0 else earlier_other, near, MASKED)
            groups.append((near, side, here))
        top = functools.reduce(
            jnp.maximum, [jnp.max(scores, axis=-1, keepdims=True) for scores, _, _ in groups]
        )
        mixed = jnp.zeros((tile, 2 * HEAD_DIM), F32)
        for scores, side, span in groups:
            weights = jnp.exp2((scores - top) * EXP2_FACTOR).astype(BF16)
            mixed += matmul(weights, values_ref[side, span, :])
        out_ref[here, :] = (mixed[:, :HEAD_DIM] / mixed[:, HEAD_DIM:]).astype(BF16)


def back_body(
    narrow_ref, returned_ref, place_col_ref, weight_ref, own_ref, next_ref, last_ref, far_ref
):
    length = place_col_ref.shape[0]
    parts = []
    for head in range(2):
        spot = lax.broadcasted_iota(jnp.int32, (length, SLOTS), 1)
        pick = (spot == place_col_ref[:, head : head + 1]).astype(F32).astype(BF16)
        parts.append(matmul(pick, returned_ref[head]).astype(BF16))
    attended = jnp.concatenate(parts, axis=1)
    width = own_ref.shape[1]
    groups = weight_ref.shape[1] // width
    for steps, target in ((1, next_ref), (groups - 1, last_ref), (2, far_ref), (0, own_ref)):
        group = lax.rem(narrow_ref[0] + steps, groups)
        columns = pl.ds(pl.multiple_of(group * width, width), width)
        term = matmul(attended, weight_ref[:, columns])
        target[...] = term.astype(target.dtype)


def last_body(narrow_ref, own_ref, one_ref, two_ref, three_ref, hidden_ref, out_ref):
    width = own_ref.shape[1]
    columns = pl.ds(pl.multiple_of(narrow_ref[0] * width, width), width)
    mixed = own_ref[...].astype(F32)
    for term_ref in (one_ref, two_ref, three_ref):
        mixed += term_ref[...].astype(F32)
    out_ref[...] = hidden_ref[:, columns].astype(F32) + mixed


def around(value, steps):
    count = lax.axis_size("narrow")
    return lax.ppermute(value, "narrow", [(i, (i + steps) % count) for i in range(count)])


def around_by_core(value, steps):
    count = lax.axis_size("narrow")
    pairs = [
        (w * count + n, w * count + (n + (steps if w % 2 == 0 else -steps)) % count)
        for w in range(lax.axis_size("wide"))
        for n in range(count)
    ]
    return lax.ppermute(value, ("wide", "narrow"), pairs)


def swap_cores(value):
    count = lax.axis_size("wide")
    return lax.ppermute(value, "wide", [(i, i ^ 1) for i in range(count)])


def shards(tokens, w_qk1, w_value1, w_out1, w_qk2, w_value2, w_out2, cluster_ids):
    length, width = tokens.shape
    shape = jax.ShapeDtypeStruct
    wide = lax.axis_index("wide")
    narrow = lax.axis_index("narrow")
    wide_count = lax.axis_size("wide")
    core = wide & 1
    group_width = w_qk1.shape[1]

    w_first = around_by_core(w_out1, 1)
    w_half = lax.dynamic_slice_in_dim(w_out1, core * HEAD_DIM, HEAD_DIM, 0)

    qk1, value1, tails = call(
        front_body,
        (
            shape((length, group_width), BF16),
            shape((length, group_width), BF16),
            shape((2, WINDOW, group_width), BF16),
        ),
        (tokens, w_qk1, w_value1),
        scratch=(
            pltpu.VMEM((length, width), BF16),
            pltpu.VMEM((width, group_width), BF16),
            pltpu.VMEM((width, group_width), BF16),
            pltpu.SemaphoreType.DMA((4,)),
        ),
        flops=2 * length * width * group_width * 2,
        bytes_accessed=3 * 2**20,
        space=pltpu.HBM,
        mib=53,
    )
    tails, w_half = lax.optimization_barrier((tails, w_half))
    w_far_mine = around(w_half, 2)
    before = lax.ppermute(tails, "wide", [(i, i + 1) for i in range(wide_count - 1)])
    attended1 = call(
        window_body,
        shape((length, group_width), BF16),
        (wide.reshape(1), qk1, value1, before),
        prefetch=1,
        flops=2**28,
        bytes_accessed=2**20,
    )
    attended1, cluster_ids, w_out1_later, w_qk2, w_value2 = lax.optimization_barrier(
        (attended1, cluster_ids, w_out1, w_qk2, w_value2)
    )
    w_second = swap_cores(w_first)
    w_far_other = swap_cores(w_far_mine)
    far = around(attended1, 2)
    first = around_by_core(attended1, 1)
    second = around_by_core(attended1, -1)
    place, place_col, w_out1_near, w_qk2_near, w_value2_near = call(
        place_body,
        (
            shape((2, length), jnp.int32),
            shape((length, 2), jnp.int32),
            shape(w_out1.shape, BF16),
            shape(w_qk2.shape, BF16),
            shape(w_value2.shape, BF16),
        ),
        (cluster_ids, w_out1_later, w_qk2, w_value2),
        scratch=(pltpu.VMEM((2, length), jnp.int32), pltpu.SemaphoreType.DMA((4,))),
        flops=2**26,
        bytes_accessed=2**18,
        space=pltpu.HBM,
    )
    hidden, outgoing = call(
        middle_body,
        (shape((length, width), BF16), shape((2, SLOTS, 2 * HEAD_DIM), BF16)),
        (
            core.reshape(1), tokens, attended1, first, second, far,
            w_out1_near, w_first, w_second, w_far_mine, w_far_other,
            w_qk2_near, w_value2_near, place,
        ),
        prefetch=1,
        flops=2**31,
        bytes_accessed=2**23,
    )
    per_pair = 2 * SLOTS // wide_count
    arrived = lax.all_to_all(
        outgoing.reshape(wide_count, per_pair, 2 * HEAD_DIM), "wide", 0, 0, tiled=True
    ).reshape(2 * SLOTS, 2 * HEAD_DIM)
    other = swap_cores(arrived)
    info = jnp.stack([core, (((wide >> 1) & 15) < 8).astype(jnp.int32)])
    rows = 2 * SLOTS
    answers = call(
        cluster_body,
        shape((rows, HEAD_DIM), BF16),
        (info, arrived, other),
        scratch=(
            pltpu.VMEM((2, rows, 2 * HEAD_DIM), BF16),
            pltpu.VMEM((2, rows, 2 * HEAD_DIM), BF16),
            pltpu.VMEM((rows, 2 * HEAD_DIM), BF16),
        ),
        prefetch=1,
        flops=2**30,
        bytes_accessed=2**21,
    )
    returned = lax.all_to_all(
        answers.reshape(wide_count, per_pair, HEAD_DIM), "wide", 0, 0, tiled=True
    ).reshape(2, SLOTS, HEAD_DIM)
    block = shape((length, group_width), BF16)
    own, to_next, to_last, to_far = call(
        back_body,
        (block, block, block, block),
        (narrow.reshape(1), returned, place_col, w_out2),
        prefetch=1,
        flops=2**29,
        bytes_accessed=2**21,
    )
    return call(
        last_body,
        shape((length, group_width), F32),
        (
            narrow.reshape(1), own, around(to_far, 2), around(to_next, 1),
            around(to_last, -1), hidden,
        ),
        prefetch=1,
        flops=2**22,
        bytes_accessed=2**21,
    )


def solution(mesh):
    placed = (
        P("wide", None),
        P(None, "narrow"),
        P(None, "narrow"),
        P("narrow", None),
        P(None, "narrow"),
        P(None, "narrow"),
        P("narrow", None),
        P("narrow", "wide"),
    )
    return jax.shard_map(
        shards, mesh=mesh, in_specs=placed, out_specs=P("wide", "narrow"), check_vma=False
    )
```

```python
import functools
import math

import jax
import jax.numpy as jnp
from jax import lax
from jax.experimental import pallas as pl
from jax.experimental.pallas import tpu as pltpu
from jax.sharding import PartitionSpec as P

HEAD_DIM = 128
WINDOW = 256
EPS = 1e-06
MASKED = -1e30
EXP2_FACTOR = math.log2(math.e) / math.sqrt(HEAD_DIM)
CLUSTERS = 32
SLOTS = 512
BF16 = jnp.bfloat16
F32 = jnp.float32


def call(
    body, outs, args, scratch=(), prefetch=0, flops=0, bytes_accessed=0, space=pltpu.VMEM,
    mib=20,
):
    whole = [pl.BlockSpec(memory_space=pltpu.SMEM)] * prefetch + [
        pl.BlockSpec(memory_space=space)
    ] * (len(args) - prefetch)
    return pl.pallas_call(
        body,
        out_shape=outs,
        in_specs=whole,
        out_specs=jax.tree.map(lambda _: pl.BlockSpec(memory_space=pltpu.VMEM), outs),
        scratch_shapes=list(scratch),
        compiler_params=pltpu.CompilerParams(vmem_limit_bytes=mib * 2**20),
        cost_estimate=pl.CostEstimate(
            flops=flops, bytes_accessed=bytes_accessed, transcendentals=0
        ),
    )(*args)


def rms_round(values):
    factor = lax.rsqrt(jnp.mean(values * values, axis=-1, keepdims=True) + EPS)
    return (values * factor).astype(BF16)


def matmul(left, right):
    return jnp.dot(left, right, preferred_element_type=F32)


def scores_of(query, keys):
    return lax.dot_general(query, keys, (((1,), (1,)), ((), ())), preferred_element_type=F32)


def front_body(
    tokens_any, w_qk_any, w_value_any, qk_ref, value_ref, tail_ref,
    tokens_ref, w_qk_ref, w_value_ref, sems,
):
    length = tokens_ref.shape[0]
    parts = 2
    step = length // parts
    spans = [slice(part * step, (part + 1) * step) for part in range(parts)]
    token_copies = [
        pltpu.make_async_copy(tokens_any.at[span], tokens_ref.at[span], sems.at[2 + part])
        for part, span in enumerate(spans)
    ]
    qk_copy = pltpu.make_async_copy(w_qk_any, w_qk_ref, sems.at[0])
    value_copy = pltpu.make_async_copy(w_value_any, w_value_ref, sems.at[1])
    for copy in (token_copies[0], qk_copy, value_copy, *token_copies[1:]):
        copy.start()
    for part, span in enumerate(spans):
        token_copies[part].wait()
        normed = rms_round(tokens_ref[span].astype(F32))
        if part == 0:
            qk_copy.wait()
        qk = matmul(normed, w_qk_ref[...]).astype(BF16)
        if part == 0:
            value_copy.wait()
        value = matmul(normed, w_value_ref[...]).astype(BF16)
        qk_ref[span] = qk
        value_ref[span] = value
        if part == parts - 1:
            tail_ref[0] = qk[step - WINDOW :]
            tail_ref[1] = value[step - WINDOW :]


def window_body(first_ref, qk_ref, value_ref, before_ref, out_ref):
    tile = WINDOW
    row = lax.broadcasted_iota(jnp.int32, (tile, 2 * tile), 0)
    col = lax.broadcasted_iota(jnp.int32, (tile, 2 * tile), 1)
    band = (col > row) & (col < row + WINDOW)
    at_start = first_ref[0] == 0
    opening = (band & (col >= tile)) | ((row == 0) & (col == tile))
    first_band = (jnp.logical_not(at_start) & band) | (at_start & opening)
    length = qk_ref.shape[0]
    ones = jnp.ones((2 * tile, HEAD_DIM), BF16)
    for head in range(2):
        cols = slice(head * HEAD_DIM, (head + 1) * HEAD_DIM)
        for part in range(length // tile):
            query = qk_ref[part * tile : (part + 1) * tile, cols]
            if part == 0:
                keys = jnp.concatenate([before_ref[0, :, cols], query], axis=0)
                values = jnp.concatenate([before_ref[1, :, cols], value_ref[:tile, cols]], axis=0)
            else:
                keys = qk_ref[(part - 1) * tile : (part + 1) * tile, cols]
                values = value_ref[(part - 1) * tile : (part + 1) * tile, cols]
            scores = jnp.where(first_band if part == 0 else band, scores_of(query, keys), MASKED)
            top = jnp.max(scores, axis=-1, keepdims=True)
            weights = jnp.exp2((scores - top) * EXP2_FACTOR).astype(BF16)
            mixed = matmul(weights, jnp.concatenate([values, ones], axis=1))
            out_ref[part * tile : (part + 1) * tile, cols] = (
                mixed[:, :HEAD_DIM] / mixed[:, HEAD_DIM:]
            ).astype(BF16)


def place_body(
    ids_any, w_out_any, w_qk_any, w_value_any,
    place_ref, place_col_ref, w_out_ref, w_qk_ref, w_value_ref, ids_ref, sems,
):
    copies = [
        pltpu.make_async_copy(source, target, sems.at[index])
        for index, (source, target) in enumerate(
            (
                (ids_any, ids_ref), (w_out_any, w_out_ref),
                (w_qk_any, w_qk_ref), (w_value_any, w_value_ref),
            )
        )
    ]
    for copy in copies:
        copy.start()
    copies[0].wait()
    length = ids_ref.shape[1]
    earlier = (
        lax.broadcasted_iota(jnp.int32, (length, length), 0)
        < lax.broadcasted_iota(jnp.int32, (length, length), 1)
    ).astype(F32).astype(BF16)
    same = lax.broadcasted_iota(jnp.int32, (length, length), 0) == lax.broadcasted_iota(
        jnp.int32, (length, length), 1
    )
    lower = (
        lax.broadcasted_iota(jnp.int32, (CLUSTERS, CLUSTERS), 1)
        < lax.broadcasted_iota(jnp.int32, (CLUSTERS, CLUSTERS), 0)
    ).astype(F32).astype(BF16)
    for head in range(2):
        ids = ids_ref[head : head + 1, :]
        match = (
            lax.broadcasted_iota(jnp.int32, (CLUSTERS, length), 0) == ids
        ).astype(F32)
        rank = matmul(match.astype(BF16), earlier)
        count = jnp.sum(match, axis=1, keepdims=True)
        count = jnp.broadcast_to(count, (CLUSTERS, 128))
        large = count > 20.0
        small = count < 10.0
        middle = jnp.logical_not(large | small)
        one = lambda kind: matmul(lower, kind.astype(F32).astype(BF16))
        at_large = one(large) * 32.0
        nth = one(middle)
        pair = jnp.floor(nth * 0.5)
        at_middle = 256.0 + pair * 32.0 + (nth - 2.0 * pair) * 12.0
        at_small = 256.0 + one(small) * 32.0 + 24.0
        base = jnp.where(large, at_large, jnp.where(small, at_small, at_middle))[:, :1]
        place = jnp.sum(match * (rank + base), axis=0, keepdims=True)
        place_ref[head : head + 1, :] = place.astype(jnp.int32)
        column = jnp.sum(jnp.where(same, place, 0.0), axis=1, keepdims=True)
        place_col_ref[:, head : head + 1] = column.astype(jnp.int32)
    for copy in copies[1:]:
        copy.wait()


def middle_body(
    core_ref,
    tokens_ref,
    own_ref,
    first_ref,
    second_ref,
    far_ref,
    w_own_ref,
    w_first_ref,
    w_second_ref,
    w_far_mine_ref,
    w_far_other_ref,
    w_qk_ref,
    w_value_ref,
    place_ref,
    hidden_ref,
    out_ref,
):
    even = core_ref[0] == 0
    far_mine = w_far_mine_ref[...]
    far_other = w_far_other_ref[...]
    left_side = [own_ref[...], first_ref[...], second_ref[...], far_ref[...]]
    right_side = [
        w_own_ref[...],
        w_first_ref[...],
        w_second_ref[...],
        jnp.where(even, far_mine, far_other),
        jnp.where(even, far_other, far_mine),
    ]
    mixed = matmul(jnp.concatenate(left_side, axis=1), jnp.concatenate(right_side, axis=0))
    hidden = (tokens_ref[...].astype(F32) + mixed).astype(BF16)
    hidden_ref[...] = hidden
    normed = rms_round(hidden.astype(F32))
    qk = matmul(normed, w_qk_ref[...]).astype(BF16)
    value = matmul(normed, w_value_ref[...]).astype(BF16)
    length = qk.shape[0]
    for head in range(2):
        cols = slice(head * HEAD_DIM, (head + 1) * HEAD_DIM)
        spot = lax.broadcasted_iota(jnp.int32, (SLOTS, length), 0)
        pick = (spot == place_ref[head : head + 1, :]).astype(F32).astype(BF16)
        rows = jnp.concatenate([qk[:, cols], value[:, cols]], axis=1)
        out_ref[head] = matmul(pick, rows).astype(BF16)


def segments(tile, which, whole):
    slot = (lax.broadcasted_iota(jnp.int32, (tile, HEAD_DIM), 0) & 15) + 16 * which
    found = jnp.where(slot >= 24, 2, jnp.where(slot >= 12, 1, 0))
    return jnp.where(whole, 0, found)


def side_scores(query_ref, key_ref, part, tile, core, key_core, whole, keep):
    lane = lax.broadcasted_iota(jnp.int32, (tile, HEAD_DIM), 1)
    fence = jnp.where(lane == segments(tile, core, whole), 0.0, MASKED).astype(BF16)
    member = jnp.where(lane == segments(tile, key_core, whole), 1.0, 0.0).astype(BF16)
    here = slice(part * tile, (part + 1) * tile)
    query = jnp.concatenate([query_ref[here, :HEAD_DIM], fence], axis=1)
    groups = []
    for past in range(part + 1):
        span = slice(past * tile, (past + 1) * tile)
        keys = jnp.concatenate([key_ref[span, :HEAD_DIM], member], axis=1)
        scores = scores_of(query, keys)
        if past == part:
            scores = jnp.where(keep, scores, MASKED)
        groups.append(scores)
    return groups


def row_tops(groups):
    joined = functools.reduce(jnp.maximum, groups)
    return jnp.max(joined, axis=-1, keepdims=True)


def weigh(groups, top, value_ref, tile):
    ones = jnp.ones((tile, HEAD_DIM), BF16)
    mixed = None
    for past, scores in enumerate(groups):
        weights = jnp.exp2((scores - top) * EXP2_FACTOR).astype(BF16)
        values = value_ref[past * tile : (past + 1) * tile, HEAD_DIM:]
        term = matmul(weights, jnp.concatenate([values, ones], axis=1))
        mixed = term if mixed is None else mixed + term
    return mixed


def own_side_body(info_ref, mine_ref, mixed_ref, top_ref):
    core = info_ref[0]
    whole = info_ref[1] == 1
    tile = 256
    row = lax.broadcasted_iota(jnp.int32, (tile, tile), 0)
    col = lax.broadcasted_iota(jnp.int32, (tile, tile), 1)
    earlier = col < row
    slot = (row & 15) + 16 * core
    opens = (slot == 0) | (jnp.logical_not(whole) & ((slot == 12) | (slot == 24)))
    alone = (row == col) & opens & (row < 16)
    for part in range(mine_ref.shape[0] // tile):
        here = slice(part * tile, (part + 1) * tile)
        keep = (earlier | alone) if part == 0 else earlier
        groups = side_scores(mine_ref, mine_ref, part, tile, core, core, whole, keep)
        top = row_tops(groups)
        mixed_ref[here, :] = weigh(groups, top, mine_ref, tile)
        top_ref[here, :] = jnp.broadcast_to(top, (tile, HEAD_DIM))


def other_side_body(info_ref, mine_ref, other_ref, mixed_ref, top_ref, out_ref):
    core = info_ref[0]
    whole = info_ref[1] == 1
    tile = 256
    row = lax.broadcasted_iota(jnp.int32, (tile, tile), 0)
    col = lax.broadcasted_iota(jnp.int32, (tile, tile), 1)
    earlier = (col >> 4) < (row >> 4) + core
    for part in range(mine_ref.shape[0] // tile):
        here = slice(part * tile, (part + 1) * tile)
        groups = side_scores(mine_ref, other_ref, part, tile, core, 1 - core, whole, earlier)
        own_top = top_ref[here, :]
        top = jnp.maximum(jnp.broadcast_to(row_tops(groups), (tile, HEAD_DIM)), own_top)
        shrink = jnp.exp2((own_top - top) * EXP2_FACTOR)
        mixed = weigh(groups, jnp.concatenate([top, top], axis=1), other_ref, tile)
        total = mixed[:, HEAD_DIM:] + mixed_ref[here, HEAD_DIM:] * shrink
        sums = mixed[:, :HEAD_DIM] + mixed_ref[here, :HEAD_DIM] * shrink
        out_ref[here, :] = (sums / total).astype(BF16)


def back_body(
    narrow_ref, returned_ref, place_col_ref, weight_ref, own_ref, next_ref, last_ref, far_ref
):
    length = place_col_ref.shape[0]
    parts = []
    for head in range(2):
        spot = lax.broadcasted_iota(jnp.int32, (length, SLOTS), 1)
        pick = (spot == place_col_ref[:, head : head + 1]).astype(F32).astype(BF16)
        parts.append(matmul(pick, returned_ref[head]).astype(BF16))
    attended = jnp.concatenate(parts, axis=1)
    width = own_ref.shape[1]
    groups = weight_ref.shape[1] // width
    for steps, target in ((1, next_ref), (groups - 1, last_ref), (2, far_ref), (0, own_ref)):
        group = lax.rem(narrow_ref[0] + steps, groups)
        columns = pl.ds(pl.multiple_of(group * width, width), width)
        term = matmul(attended, weight_ref[:, columns])
        target[...] = term.astype(target.dtype)


def last_body(narrow_ref, own_ref, one_ref, two_ref, three_ref, hidden_ref, out_ref):
    width = own_ref.shape[1]
    columns = pl.ds(pl.multiple_of(narrow_ref[0] * width, width), width)
    mixed = own_ref[...].astype(F32)
    for term_ref in (one_ref, two_ref, three_ref):
        mixed += term_ref[...].astype(F32)
    out_ref[...] = hidden_ref[:, columns].astype(F32) + mixed


def around(value, steps):
    count = lax.axis_size("narrow")
    return lax.ppermute(value, "narrow", [(i, (i + steps) % count) for i in range(count)])


def around_by_core(value, steps):
    count = lax.axis_size("narrow")
    pairs = [
        (w * count + n, w * count + (n + (steps if w % 2 == 0 else -steps)) % count)
        for w in range(lax.axis_size("wide"))
        for n in range(count)
    ]
    return lax.ppermute(value, ("wide", "narrow"), pairs)


def swap_cores(value):
    count = lax.axis_size("wide")
    return lax.ppermute(value, "wide", [(i, i ^ 1) for i in range(count)])


def shards(tokens, w_qk1, w_value1, w_out1, w_qk2, w_value2, w_out2, cluster_ids):
    length, width = tokens.shape
    shape = jax.ShapeDtypeStruct
    wide = lax.axis_index("wide")
    narrow = lax.axis_index("narrow")
    wide_count = lax.axis_size("wide")
    core = wide & 1
    group_width = w_qk1.shape[1]

    w_first = around_by_core(w_out1, 1)
    w_half = lax.dynamic_slice_in_dim(w_out1, core * HEAD_DIM, HEAD_DIM, 0)

    qk1, value1, tails = call(
        front_body,
        (
            shape((length, group_width), BF16),
            shape((length, group_width), BF16),
            shape((2, WINDOW, group_width), BF16),
        ),
        (tokens, w_qk1, w_value1),
        scratch=(
            pltpu.VMEM((length, width), BF16),
            pltpu.VMEM((width, group_width), BF16),
            pltpu.VMEM((width, group_width), BF16),
            pltpu.SemaphoreType.DMA((4,)),
        ),
        flops=2 * length * width * group_width * 2,
        bytes_accessed=3 * 2**20,
        space=pltpu.HBM,
        mib=53,
    )
    tails, w_half = lax.optimization_barrier((tails, w_half))
    w_far_mine = around(w_half, 2)
    before = lax.ppermute(tails, "wide", [(i, i + 1) for i in range(wide_count - 1)])
    attended1 = call(
        window_body,
        shape((length, group_width), BF16),
        (wide.reshape(1), qk1, value1, before),
        prefetch=1,
        flops=2**28,
        bytes_accessed=2**20,
    )
    attended1, cluster_ids, w_out1_later, w_qk2, w_value2 = lax.optimization_barrier(
        (attended1, cluster_ids, w_out1, w_qk2, w_value2)
    )
    w_second = swap_cores(w_first)
    w_far_other = swap_cores(w_far_mine)
    far = around(attended1, 2)
    first = around_by_core(attended1, 1)
    second = around_by_core(attended1, -1)
    place, place_col, w_out1_near, w_qk2_near, w_value2_near = call(
        place_body,
        (
            shape((2, length), jnp.int32),
            shape((length, 2), jnp.int32),
            shape(w_out1.shape, BF16),
            shape(w_qk2.shape, BF16),
            shape(w_value2.shape, BF16),
        ),
        (cluster_ids, w_out1_later, w_qk2, w_value2),
        scratch=(pltpu.VMEM((2, length), jnp.int32), pltpu.SemaphoreType.DMA((4,))),
        flops=2**26,
        bytes_accessed=2**18,
        space=pltpu.HBM,
    )
    hidden, outgoing = call(
        middle_body,
        (shape((length, width), BF16), shape((2, SLOTS, 2 * HEAD_DIM), BF16)),
        (
            core.reshape(1), tokens, attended1, first, second, far,
            w_out1_near, w_first, w_second, w_far_mine, w_far_other,
            w_qk2_near, w_value2_near, place,
        ),
        prefetch=1,
        flops=2**31,
        bytes_accessed=2**23,
    )
    per_pair = 2 * SLOTS // wide_count
    arrived = lax.all_to_all(
        outgoing.reshape(wide_count, per_pair, 2 * HEAD_DIM), "wide", 0, 0, tiled=True
    ).reshape(2 * SLOTS, 2 * HEAD_DIM)
    other = swap_cores(arrived)
    info = jnp.stack([core, (((wide >> 1) & 15) < 8).astype(jnp.int32)])
    rows = 2 * SLOTS
    own_mixed, own_top = call(
        own_side_body,
        (shape((rows, 2 * HEAD_DIM), F32), shape((rows, HEAD_DIM), F32)),
        (info, arrived),
        prefetch=1,
        flops=2**30,
        bytes_accessed=2**21,
    )
    answers = call(
        other_side_body,
        shape((rows, HEAD_DIM), BF16),
        (info, arrived, other, own_mixed, own_top),
        prefetch=1,
        flops=2**30,
        bytes_accessed=2**21,
    )
    returned = lax.all_to_all(
        answers.reshape(wide_count, per_pair, HEAD_DIM), "wide", 0, 0, tiled=True
    ).reshape(2, SLOTS, HEAD_DIM)
    block = shape((length, group_width), BF16)
    own, to_next, to_last, to_far = call(
        back_body,
        (block, block, block, block),
        (narrow.reshape(1), returned, place_col, w_out2),
        prefetch=1,
        flops=2**29,
        bytes_accessed=2**21,
    )
    return call(
        last_body,
        shape((length, group_width), F32),
        (
            narrow.reshape(1), own, around(to_far, 2), around(to_next, 1),
            around(to_last, -1), hidden,
        ),
        prefetch=1,
        flops=2**22,
        bytes_accessed=2**21,
    )


def solution(mesh):
    placed = (
        P("wide", None),
        P(None, "narrow"),
        P(None, "narrow"),
        P("narrow", None),
        P(None, "narrow"),
        P(None, "narrow"),
        P("narrow", None),
        P("narrow", "wide"),
    )
    return jax.shard_map(
        shards, mesh=mesh, in_specs=placed, out_specs=P("wide", "narrow"), check_vma=False
    )
```

```python
import functools
import math

import jax
import jax.numpy as jnp
from jax import lax
from jax.experimental import pallas as pl
from jax.experimental.pallas import tpu as pltpu
from jax.sharding import PartitionSpec as P

HEAD_DIM = 128
WINDOW = 256
EPS = 1e-06
MASKED = -1e30
EXP2_FACTOR = math.log2(math.e) / math.sqrt(HEAD_DIM)
CLUSTERS = 32
SLOTS = 512
BF16 = jnp.bfloat16
F32 = jnp.float32


def call(
    body, outs, args, scratch=(), prefetch=0, flops=0, bytes_accessed=0, space=pltpu.VMEM,
    mib=20,
    out_space=pltpu.VMEM,
):
    whole = [pl.BlockSpec(memory_space=pltpu.SMEM)] * prefetch + [
        pl.BlockSpec(memory_space=space)
    ] * (len(args) - prefetch)
    return pl.pallas_call(
        body,
        out_shape=outs,
        in_specs=whole,
        out_specs=jax.tree.map(lambda _: pl.BlockSpec(memory_space=out_space), outs),
        scratch_shapes=list(scratch),
        compiler_params=pltpu.CompilerParams(vmem_limit_bytes=mib * 2**20),
        cost_estimate=pl.CostEstimate(
            flops=flops, bytes_accessed=bytes_accessed, transcendentals=0
        ),
    )(*args)


def rms_round(values):
    factor = lax.rsqrt(jnp.mean(values * values, axis=-1, keepdims=True) + EPS)
    return (values * factor).astype(BF16)


def matmul(left, right):
    return jnp.dot(left, right, preferred_element_type=F32)


def scores_of(query, keys):
    return lax.dot_general(query, keys, (((1,), (1,)), ((), ())), preferred_element_type=F32)


def front_body(
    tokens_any, w_qk_any, w_value_any, qk_ref, value_ref, tail_ref,
    tokens_ref, w_qk_ref, w_value_ref, sems,
):
    length = tokens_ref.shape[0]
    parts = 2
    step = length // parts
    spans = [slice(part * step, (part + 1) * step) for part in range(parts)]
    token_copies = [
        pltpu.make_async_copy(tokens_any.at[span], tokens_ref.at[span], sems.at[2 + part])
        for part, span in enumerate(spans)
    ]
    qk_copy = pltpu.make_async_copy(w_qk_any, w_qk_ref, sems.at[0])
    value_copy = pltpu.make_async_copy(w_value_any, w_value_ref, sems.at[1])
    for copy in (token_copies[0], qk_copy, value_copy, *token_copies[1:]):
        copy.start()
    for part, span in enumerate(spans):
        token_copies[part].wait()
        normed = rms_round(tokens_ref[span].astype(F32))
        if part == 0:
            qk_copy.wait()
        qk = matmul(normed, w_qk_ref[...]).astype(BF16)
        if part == 0:
            value_copy.wait()
        value = matmul(normed, w_value_ref[...]).astype(BF16)
        qk_ref[span] = qk
        value_ref[span] = value
        if part == parts - 1:
            tail_ref[0] = qk[step - WINDOW :]
            tail_ref[1] = value[step - WINDOW :]


def window_body(first_ref, qk_ref, value_ref, before_ref, out_ref):
    tile = WINDOW
    row = lax.broadcasted_iota(jnp.int32, (tile, 2 * tile), 0)
    col = lax.broadcasted_iota(jnp.int32, (tile, 2 * tile), 1)
    band = (col > row) & (col < row + WINDOW)
    at_start = first_ref[0] == 0
    opening = (band & (col >= tile)) | ((row == 0) & (col == tile))
    first_band = (jnp.logical_not(at_start) & band) | (at_start & opening)
    length = qk_ref.shape[0]
    ones = jnp.ones((2 * tile, HEAD_DIM), BF16)
    pieces = []
    for head in range(2):
        cols = slice(head * HEAD_DIM, (head + 1) * HEAD_DIM)
        for part in range(length // tile):
            here = slice(part * tile, (part + 1) * tile)
            query = qk_ref[here, cols]
            if part == 0:
                keys = jnp.concatenate([before_ref[0, :, cols], query], axis=0)
                values = jnp.concatenate([before_ref[1, :, cols], value_ref[:tile, cols]], axis=0)
            else:
                keys = qk_ref[(part - 1) * tile : (part + 1) * tile, cols]
                values = value_ref[(part - 1) * tile : (part + 1) * tile, cols]
            keep = first_band if part == 0 else band
            scores = jnp.where(keep, scores_of(query, keys), MASKED)
            pieces.append((here, cols, values, scores, jnp.max(scores, axis=-1, keepdims=True)))
    for here, cols, values, scores, top in pieces:
        weights = jnp.exp2((scores - top) * EXP2_FACTOR).astype(BF16)
        mixed = matmul(weights, jnp.concatenate([values, ones], axis=1))
        out_ref[here, cols] = (mixed[:, :HEAD_DIM] / mixed[:, HEAD_DIM:]).astype(BF16)


def place_body(
    ids_any, w_out_any, w_qk_any, w_value_any,
    place_ref, place_col_ref, w_out_ref, w_qk_ref, w_value_ref, ids_ref, sems,
):
    copies = [
        pltpu.make_async_copy(source, target, sems.at[index])
        for index, (source, target) in enumerate(
            (
                (ids_any, ids_ref), (w_out_any, w_out_ref),
                (w_qk_any, w_qk_ref), (w_value_any, w_value_ref),
            )
        )
    ]
    for copy in copies:
        copy.start()
    copies[0].wait()
    length = ids_ref.shape[1]
    earlier = (
        lax.broadcasted_iota(jnp.int32, (length, length), 0)
        < lax.broadcasted_iota(jnp.int32, (length, length), 1)
    ).astype(F32).astype(BF16)
    same = lax.broadcasted_iota(jnp.int32, (length, length), 0) == lax.broadcasted_iota(
        jnp.int32, (length, length), 1
    )
    lower = (
        lax.broadcasted_iota(jnp.int32, (CLUSTERS, CLUSTERS), 1)
        < lax.broadcasted_iota(jnp.int32, (CLUSTERS, CLUSTERS), 0)
    ).astype(F32).astype(BF16)
    for head in range(2):
        ids = ids_ref[head : head + 1, :]
        match = (
            lax.broadcasted_iota(jnp.int32, (CLUSTERS, length), 0) == ids
        ).astype(F32)
        rank = matmul(match.astype(BF16), earlier)
        count = jnp.sum(match, axis=1, keepdims=True)
        count = jnp.broadcast_to(count, (CLUSTERS, 128))
        large = count > 20.0
        small = count < 10.0
        middle = jnp.logical_not(large | small)
        one = lambda kind: matmul(lower, kind.astype(F32).astype(BF16))
        at_large = one(large) * 32.0
        nth = one(middle)
        pair = jnp.floor(nth * 0.5)
        at_middle = 256.0 + pair * 32.0 + (nth - 2.0 * pair) * 12.0
        at_small = 256.0 + one(small) * 32.0 + 24.0
        base = jnp.where(large, at_large, jnp.where(small, at_small, at_middle))[:, :1]
        place = jnp.sum(match * (rank + base), axis=0, keepdims=True)
        place_ref[head : head + 1, :] = place.astype(jnp.int32)
        column = jnp.sum(jnp.where(same, place, 0.0), axis=1, keepdims=True)
        place_col_ref[:, head : head + 1] = column.astype(jnp.int32)
    for copy in copies[1:]:
        copy.wait()


def begin_mixed_body(
    core_ref, tokens_ref, own_ref, far_ref, w_own_ref, w_far_mine_ref, w_far_other_ref, started_ref
):
    even = core_ref[0] == 0
    far_mine = w_far_mine_ref[...]
    far_other = w_far_other_ref[...]
    left_side = jnp.concatenate([own_ref[...], far_ref[...]], axis=1)
    right_side = [
        w_own_ref[...],
        jnp.where(even, far_mine, far_other),
        jnp.where(even, far_other, far_mine),
    ]
    mixed = matmul(left_side, jnp.concatenate(right_side, axis=0))
    started_ref[...] = tokens_ref[...].astype(F32) + mixed


def middle_body(
    started_ref,
    first_ref,
    second_ref,
    w_first_ref,
    w_second_ref,
    w_qk_ref,
    w_value_ref,
    place_ref,
    hidden_ref,
    out_ref,
):
    left_side = jnp.concatenate([first_ref[...], second_ref[...]], axis=1)
    right_side = jnp.concatenate([w_first_ref[...], w_second_ref[...]], axis=0)
    hidden = (started_ref[...] + matmul(left_side, right_side)).astype(BF16)
    hidden_ref[...] = hidden
    normed = rms_round(hidden.astype(F32))
    qk = matmul(normed, w_qk_ref[...]).astype(BF16)
    value = matmul(normed, w_value_ref[...]).astype(BF16)
    length = qk.shape[0]
    for head in range(2):
        cols = slice(head * HEAD_DIM, (head + 1) * HEAD_DIM)
        spot = lax.broadcasted_iota(jnp.int32, (SLOTS, length), 0)
        pick = (spot == place_ref[head : head + 1, :]).astype(F32).astype(BF16)
        rows = jnp.concatenate([qk[:, cols], value[:, cols]], axis=1)
        out_ref[head] = matmul(pick, rows).astype(BF16)


def segments(tile, which, whole):
    slot = (lax.broadcasted_iota(jnp.int32, (tile, HEAD_DIM), 0) & 15) + 16 * which
    found = jnp.where(slot >= 24, 2, jnp.where(slot >= 12, 1, 0))
    return jnp.where(whole, 0, found)


def side_scores(query_ref, key_ref, part, tile, core, key_core, whole, keep):
    lane = lax.broadcasted_iota(jnp.int32, (tile, HEAD_DIM), 1)
    fence = jnp.where(lane == segments(tile, core, whole), 0.0, MASKED).astype(BF16)
    member = jnp.where(lane == segments(tile, key_core, whole), 1.0, 0.0).astype(BF16)
    here = slice(part * tile, (part + 1) * tile)
    query = jnp.concatenate([query_ref[here, :HEAD_DIM], fence], axis=1)
    groups = []
    for past in range(part + 1):
        span = slice(past * tile, (past + 1) * tile)
        keys = jnp.concatenate([key_ref[span, :HEAD_DIM], member], axis=1)
        scores = scores_of(query, keys)
        if past == part:
            scores = jnp.where(keep, scores, MASKED)
        groups.append(scores)
    return groups


def row_tops(groups):
    joined = functools.reduce(jnp.maximum, groups)
    return jnp.max(joined, axis=-1, keepdims=True)


def weigh(groups, top, value_ref, tile):
    ones = jnp.ones((tile, HEAD_DIM), BF16)
    mixed = None
    for past, scores in enumerate(groups):
        weights = jnp.exp2((scores - top) * EXP2_FACTOR).astype(BF16)
        values = value_ref[past * tile : (past + 1) * tile, HEAD_DIM:]
        term = matmul(weights, jnp.concatenate([values, ones], axis=1))
        mixed = term if mixed is None else mixed + term
    return mixed


def own_side_body(info_ref, mine_ref, mixed_ref, top_ref):
    core = info_ref[0]
    whole = info_ref[1] == 1
    tile = 256
    row = lax.broadcasted_iota(jnp.int32, (tile, tile), 0)
    col = lax.broadcasted_iota(jnp.int32, (tile, tile), 1)
    earlier = col < row
    slot = (row & 15) + 16 * core
    opens = (slot == 0) | (jnp.logical_not(whole) & ((slot == 12) | (slot == 24)))
    alone = (row == col) & opens & (row < 16)
    parts = range(mine_ref.shape[0] // tile)
    scored = [
        side_scores(
            mine_ref, mine_ref, part, tile, core, core, whole,
            (earlier | alone) if part == 0 else earlier,
        )
        for part in parts
    ]
    tops = [row_tops(groups) for groups in scored]
    for part in parts:
        here = slice(part * tile, (part + 1) * tile)
        top = tops[part]
        mixed_ref[here, :] = weigh(scored[part], top, mine_ref, tile)
        top_ref[here, :] = jnp.broadcast_to(top, (tile, HEAD_DIM))


def other_side_body(info_ref, mine_ref, other_ref, mixed_ref, top_ref, out_ref):
    core = info_ref[0]
    whole = info_ref[1] == 1
    tile = 256
    row = lax.broadcasted_iota(jnp.int32, (tile, tile), 0)
    col = lax.broadcasted_iota(jnp.int32, (tile, tile), 1)
    earlier = (col >> 4) < (row >> 4) + core
    parts = range(mine_ref.shape[0] // tile)
    scored = [
        side_scores(mine_ref, other_ref, part, tile, core, 1 - core, whole, earlier)
        for part in parts
    ]
    tops = [row_tops(groups) for groups in scored]
    for part in parts:
        here = slice(part * tile, (part + 1) * tile)
        own_top = top_ref[here, :]
        top = jnp.maximum(jnp.broadcast_to(tops[part], (tile, HEAD_DIM)), own_top)
        shrink = jnp.exp2((own_top - top) * EXP2_FACTOR)
        mixed = weigh(scored[part], jnp.concatenate([top, top], axis=1), other_ref, tile)
        total = mixed[:, HEAD_DIM:] + mixed_ref[here, HEAD_DIM:] * shrink
        sums = mixed[:, :HEAD_DIM] + mixed_ref[here, :HEAD_DIM] * shrink
        out_ref[here, :] = (sums / total).astype(BF16)


def back_body(
    narrow_ref, returned_ref, place_col_ref, weight_ref, own_ref, next_ref, last_ref, far_ref
):
    length = place_col_ref.shape[0]
    parts = []
    for head in range(2):
        spot = lax.broadcasted_iota(jnp.int32, (length, SLOTS), 1)
        pick = (spot == place_col_ref[:, head : head + 1]).astype(F32).astype(BF16)
        parts.append(matmul(pick, returned_ref[head]).astype(BF16))
    attended = jnp.concatenate(parts, axis=1)
    width = own_ref.shape[1]
    groups = weight_ref.shape[1] // width
    for steps, target in ((1, next_ref), (groups - 1, last_ref), (2, far_ref), (0, own_ref)):
        group = lax.rem(narrow_ref[0] + steps, groups)
        columns = pl.ds(pl.multiple_of(group * width, width), width)
        term = matmul(attended, weight_ref[:, columns])
        target[...] = term.astype(target.dtype)


def last_body(
    narrow_ref, own_ref, one_ref, two_ref, three_ref, hidden_ref, out_any, out_ref, sems
):
    length, width = own_ref.shape
    columns = pl.ds(pl.multiple_of(narrow_ref[0] * width, width), width)
    parts = 4
    step = length // parts
    copies = []
    for part in range(parts):
        here = slice(part * step, (part + 1) * step)
        mixed = own_ref[here, :].astype(F32)
        for term_ref in (one_ref, two_ref, three_ref):
            mixed += term_ref[here, :].astype(F32)
        out_ref[here, :] = hidden_ref[here, columns].astype(F32) + mixed
        copy = pltpu.make_async_copy(out_ref.at[here], out_any.at[here], sems.at[part])
        copy.start()
        copies.append(copy)
    for copy in copies:
        copy.wait()


def around(value, steps):
    count = lax.axis_size("narrow")
    return lax.ppermute(value, "narrow", [(i, (i + steps) % count) for i in range(count)])


def around_by_core(value, steps):
    count = lax.axis_size("narrow")
    pairs = [
        (w * count + n, w * count + (n + (steps if w % 2 == 0 else -steps)) % count)
        for w in range(lax.axis_size("wide"))
        for n in range(count)
    ]
    return lax.ppermute(value, ("wide", "narrow"), pairs)


def swap_cores(value):
    count = lax.axis_size("wide")
    return lax.ppermute(value, "wide", [(i, i ^ 1) for i in range(count)])


def shards(tokens, w_qk1, w_value1, w_out1, w_qk2, w_value2, w_out2, cluster_ids):
    length, width = tokens.shape
    shape = jax.ShapeDtypeStruct
    wide = lax.axis_index("wide")
    narrow = lax.axis_index("narrow")
    wide_count = lax.axis_size("wide")
    core = wide & 1
    group_width = w_qk1.shape[1]

    w_first = around_by_core(w_out1, 1)
    w_half = lax.dynamic_slice_in_dim(w_out1, core * HEAD_DIM, HEAD_DIM, 0)

    qk1, value1, tails = call(
        front_body,
        (
            shape((length, group_width), BF16),
            shape((length, group_width), BF16),
            shape((2, WINDOW, group_width), BF16),
        ),
        (tokens, w_qk1, w_value1),
        scratch=(
            pltpu.VMEM((length, width), BF16),
            pltpu.VMEM((width, group_width), BF16),
            pltpu.VMEM((width, group_width), BF16),
            pltpu.SemaphoreType.DMA((4,)),
        ),
        flops=2 * length * width * group_width * 2,
        bytes_accessed=3 * 2**20,
        space=pltpu.HBM,
        mib=53,
    )
    tails, w_half = lax.optimization_barrier((tails, w_half))
    w_far_mine = around(w_half, 2)
    before = lax.ppermute(tails, "wide", [(i, i + 1) for i in range(wide_count - 1)])
    attended1 = call(
        window_body,
        shape((length, group_width), BF16),
        (wide.reshape(1), qk1, value1, before),
        prefetch=1,
        flops=2**28,
        bytes_accessed=2**20,
    )
    attended1, cluster_ids, w_out1_later, w_qk2, w_value2 = lax.optimization_barrier(
        (attended1, cluster_ids, w_out1, w_qk2, w_value2)
    )
    w_second = swap_cores(w_first)
    w_far_other = swap_cores(w_far_mine)
    far = around(attended1, 2)
    first = around_by_core(attended1, 1)
    second = around_by_core(attended1, -1)
    place, place_col, w_out1_near, w_qk2_near, w_value2_near = call(
        place_body,
        (
            shape((2, length), jnp.int32),
            shape((length, 2), jnp.int32),
            shape(w_out1.shape, BF16),
            shape(w_qk2.shape, BF16),
            shape(w_value2.shape, BF16),
        ),
        (cluster_ids, w_out1_later, w_qk2, w_value2),
        scratch=(pltpu.VMEM((2, length), jnp.int32), pltpu.SemaphoreType.DMA((4,))),
        flops=2**26,
        bytes_accessed=2**18,
        space=pltpu.HBM,
    )
    started = call(
        begin_mixed_body,
        shape((length, width), F32),
        (core.reshape(1), tokens, attended1, far, w_out1_near, w_far_mine, w_far_other),
        prefetch=1,
        flops=2**30,
        bytes_accessed=2**22,
    )
    hidden, outgoing = call(
        middle_body,
        (shape((length, width), BF16), shape((2, SLOTS, 2 * HEAD_DIM), BF16)),
        (
            started, first, second, w_first, w_second, w_qk2_near, w_value2_near, place,
        ),
        flops=2**31,
        bytes_accessed=2**23,
    )
    per_pair = 2 * SLOTS // wide_count
    arrived = lax.all_to_all(
        outgoing.reshape(wide_count, per_pair, 2 * HEAD_DIM), "wide", 0, 0, tiled=True
    ).reshape(2 * SLOTS, 2 * HEAD_DIM)
    other = swap_cores(arrived)
    info = jnp.stack([core, (((wide >> 1) & 15) < 8).astype(jnp.int32)])
    rows = 2 * SLOTS
    own_mixed, own_top = call(
        own_side_body,
        (shape((rows, 2 * HEAD_DIM), F32), shape((rows, HEAD_DIM), F32)),
        (info, arrived),
        prefetch=1,
        flops=2**30,
        bytes_accessed=2**21,
    )
    answers = call(
        other_side_body,
        shape((rows, HEAD_DIM), BF16),
        (info, arrived, other, own_mixed, own_top),
        prefetch=1,
        flops=2**30,
        bytes_accessed=2**21,
    )
    returned = lax.all_to_all(
        answers.reshape(wide_count, per_pair, HEAD_DIM), "wide", 0, 0, tiled=True
    ).reshape(2, SLOTS, HEAD_DIM)
    block = shape((length, group_width), BF16)
    own, to_next, to_last, to_far = call(
        back_body,
        (block, block, block, block),
        (narrow.reshape(1), returned, place_col, w_out2),
        prefetch=1,
        flops=2**29,
        bytes_accessed=2**21,
    )
    return call(
        last_body,
        shape((length, group_width), F32),
        (
            narrow.reshape(1), own, around(to_far, 2), around(to_next, 1),
            around(to_last, -1), hidden,
        ),
        scratch=(
            pltpu.VMEM((length, group_width), F32),
            pltpu.SemaphoreType.DMA((4,)),
        ),
        out_space=pl.ANY,
        prefetch=1,
        flops=2**22,
        bytes_accessed=2**21,
    )


def solution(mesh):
    placed = (
        P("wide", None),
        P(None, "narrow"),
        P(None, "narrow"),
        P("narrow", None),
        P(None, "narrow"),
        P(None, "narrow"),
        P("narrow", None),
        P("narrow", "wide"),
    )
    return jax.shard_map(
        shards, mesh=mesh, in_specs=placed, out_specs=P("wide", "narrow"), check_vma=False
    )
```

```python
import functools
import math

import jax
import jax.numpy as jnp
from jax import lax
from jax.experimental import pallas as pl
from jax.experimental.pallas import tpu as pltpu
from jax.sharding import PartitionSpec as P

HEAD_DIM = 128
WINDOW = 256
EPS = 1e-06
MASKED = -1e30
EXP2_FACTOR = math.log2(math.e) / math.sqrt(HEAD_DIM)
CLUSTERS = 32
SLOTS = 512
BF16 = jnp.bfloat16
F32 = jnp.float32


def call(
    body, outs, args, scratch=(), prefetch=0, flops=0, bytes_accessed=0, space=pltpu.VMEM,
    mib=20,
    out_space=pltpu.VMEM,
):
    whole = [pl.BlockSpec(memory_space=pltpu.SMEM)] * prefetch + [
        pl.BlockSpec(memory_space=space)
    ] * (len(args) - prefetch)
    return pl.pallas_call(
        body,
        out_shape=outs,
        in_specs=whole,
        out_specs=jax.tree.map(lambda _: pl.BlockSpec(memory_space=out_space), outs),
        scratch_shapes=list(scratch),
        compiler_params=pltpu.CompilerParams(vmem_limit_bytes=mib * 2**20),
        cost_estimate=pl.CostEstimate(
            flops=flops, bytes_accessed=bytes_accessed, transcendentals=0
        ),
    )(*args)


def rms_round(values):
    factor = lax.rsqrt(jnp.mean(values * values, axis=-1, keepdims=True) + EPS)
    return (values * factor).astype(BF16)


def matmul(left, right):
    return jnp.dot(left, right, preferred_element_type=F32)


def scores_of(query, keys):
    return lax.dot_general(query, keys, (((1,), (1,)), ((), ())), preferred_element_type=F32)


def front_body(
    tokens_any, w_qk_any, w_value_any, qk_ref, value_ref, tail_ref,
    tokens_ref, w_qk_ref, w_value_ref, sems,
):
    length = tokens_ref.shape[0]
    parts = 2
    step = length // parts
    spans = [slice(part * step, (part + 1) * step) for part in range(parts)]
    token_copies = [
        pltpu.make_async_copy(tokens_any.at[span], tokens_ref.at[span], sems.at[2 + part])
        for part, span in enumerate(spans)
    ]
    qk_copy = pltpu.make_async_copy(w_qk_any, w_qk_ref, sems.at[0])
    value_copy = pltpu.make_async_copy(w_value_any, w_value_ref, sems.at[1])
    for copy in (token_copies[0], qk_copy, value_copy, *token_copies[1:]):
        copy.start()
    for part, span in enumerate(spans):
        token_copies[part].wait()
        normed = rms_round(tokens_ref[span].astype(F32))
        if part == 0:
            qk_copy.wait()
        qk = matmul(normed, w_qk_ref[...]).astype(BF16)
        if part == 0:
            value_copy.wait()
        value = matmul(normed, w_value_ref[...]).astype(BF16)
        qk_ref[span] = qk
        value_ref[span] = value
        if part == parts - 1:
            tail_ref[0] = qk[step - WINDOW :]
            tail_ref[1] = value[step - WINDOW :]


def window_body(first_ref, qk_ref, value_ref, before_ref, out_ref):
    tile = WINDOW
    row = lax.broadcasted_iota(jnp.int32, (tile, 2 * tile), 0)
    col = lax.broadcasted_iota(jnp.int32, (tile, 2 * tile), 1)
    band = (col > row) & (col < row + WINDOW)
    at_start = first_ref[0] == 0
    opening = (band & (col >= tile)) | ((row == 0) & (col == tile))
    first_band = (jnp.logical_not(at_start) & band) | (at_start & opening)
    length = qk_ref.shape[0]
    ones = jnp.ones((2 * tile, HEAD_DIM), BF16)
    pieces = []
    for head in range(2):
        cols = slice(head * HEAD_DIM, (head + 1) * HEAD_DIM)
        for part in range(length // tile):
            here = slice(part * tile, (part + 1) * tile)
            query = qk_ref[here, cols]
            if part == 0:
                keys = jnp.concatenate([before_ref[0, :, cols], query], axis=0)
                values = jnp.concatenate([before_ref[1, :, cols], value_ref[:tile, cols]], axis=0)
            else:
                keys = qk_ref[(part - 1) * tile : (part + 1) * tile, cols]
                values = value_ref[(part - 1) * tile : (part + 1) * tile, cols]
            keep = first_band if part == 0 else band
            scores = jnp.where(keep, scores_of(query, keys), MASKED)
            pieces.append((here, cols, values, scores, jnp.max(scores, axis=-1, keepdims=True)))
    for here, cols, values, scores, top in pieces:
        weights = jnp.exp2((scores - top) * EXP2_FACTOR).astype(BF16)
        mixed = matmul(weights, jnp.concatenate([values, ones], axis=1))
        out_ref[here, cols] = (mixed[:, :HEAD_DIM] / mixed[:, HEAD_DIM:]).astype(BF16)


def place_body(
    ids_any, w_out_any, w_qk_any, w_value_any,
    place_ref, place_col_ref, w_out_ref, w_qk_ref, w_value_ref, ids_ref, sems,
):
    copies = [
        pltpu.make_async_copy(source, target, sems.at[index])
        for index, (source, target) in enumerate(
            (
                (ids_any, ids_ref), (w_out_any, w_out_ref),
                (w_qk_any, w_qk_ref), (w_value_any, w_value_ref),
            )
        )
    ]
    for copy in copies:
        copy.start()
    copies[0].wait()
    length = ids_ref.shape[1]
    earlier = (
        lax.broadcasted_iota(jnp.int32, (length, length), 0)
        < lax.broadcasted_iota(jnp.int32, (length, length), 1)
    ).astype(F32).astype(BF16)
    same = lax.broadcasted_iota(jnp.int32, (length, length), 0) == lax.broadcasted_iota(
        jnp.int32, (length, length), 1
    )
    lower = (
        lax.broadcasted_iota(jnp.int32, (CLUSTERS, CLUSTERS), 1)
        < lax.broadcasted_iota(jnp.int32, (CLUSTERS, CLUSTERS), 0)
    ).astype(F32).astype(BF16)
    for head in range(2):
        ids = ids_ref[head : head + 1, :]
        match = (
            lax.broadcasted_iota(jnp.int32, (CLUSTERS, length), 0) == ids
        ).astype(F32)
        rank = matmul(match.astype(BF16), earlier)
        count = jnp.sum(match, axis=1, keepdims=True)
        count = jnp.broadcast_to(count, (CLUSTERS, 128))
        large = count > 20.0
        small = count < 10.0
        middle = jnp.logical_not(large | small)
        one = lambda kind: matmul(lower, kind.astype(F32).astype(BF16))
        at_large = one(large) * 32.0
        nth = one(middle)
        pair = jnp.floor(nth * 0.5)
        at_middle = 256.0 + pair * 32.0 + (nth - 2.0 * pair) * 12.0
        at_small = 256.0 + one(small) * 32.0 + 24.0
        base = jnp.where(large, at_large, jnp.where(small, at_small, at_middle))[:, :1]
        place = jnp.sum(match * (rank + base), axis=0, keepdims=True)
        place_ref[head : head + 1, :] = place.astype(jnp.int32)
        column = jnp.sum(jnp.where(same, place, 0.0), axis=1, keepdims=True)
        place_col_ref[:, head : head + 1] = column.astype(jnp.int32)
    for copy in copies[1:]:
        copy.wait()


def begin_mixed_body(
    core_ref, tokens_ref, own_ref, far_ref, w_own_ref, w_far_mine_ref, w_far_other_ref, started_ref
):
    even = core_ref[0] == 0
    far_mine = w_far_mine_ref[...]
    far_other = w_far_other_ref[...]
    left_side = jnp.concatenate([own_ref[...], far_ref[...]], axis=1)
    right_side = [
        w_own_ref[...],
        jnp.where(even, far_mine, far_other),
        jnp.where(even, far_other, far_mine),
    ]
    mixed = matmul(left_side, jnp.concatenate(right_side, axis=0))
    started_ref[...] = tokens_ref[...].astype(F32) + mixed


def middle_body(
    started_ref,
    first_ref,
    second_ref,
    w_first_ref,
    w_second_ref,
    w_qk_ref,
    w_value_ref,
    place_ref,
    hidden_ref,
    out_ref,
):
    left_side = jnp.concatenate([first_ref[...], second_ref[...]], axis=1)
    right_side = jnp.concatenate([w_first_ref[...], w_second_ref[...]], axis=0)
    hidden = (started_ref[...] + matmul(left_side, right_side)).astype(BF16)
    hidden_ref[...] = hidden
    normed = rms_round(hidden.astype(F32))
    qk = matmul(normed, w_qk_ref[...]).astype(BF16)
    value = matmul(normed, w_value_ref[...]).astype(BF16)
    length = qk.shape[0]
    for head in range(2):
        cols = slice(head * HEAD_DIM, (head + 1) * HEAD_DIM)
        spot = lax.broadcasted_iota(jnp.int32, (SLOTS, length), 0)
        pick = (spot == place_ref[head : head + 1, :]).astype(F32).astype(BF16)
        rows = jnp.concatenate([qk[:, cols], value[:, cols]], axis=1)
        out_ref[head] = matmul(pick, rows).astype(BF16)


def segments(tile, which, whole):
    slot = (lax.broadcasted_iota(jnp.int32, (tile, HEAD_DIM), 0) & 15) + 16 * which
    found = jnp.where(slot >= 24, 2, jnp.where(slot >= 12, 1, 0))
    return jnp.where(whole, 0, found)


def side_scores(query_ref, key_ref, part, tile, core, key_core, whole, keep):
    lane = lax.broadcasted_iota(jnp.int32, (tile, HEAD_DIM), 1)
    fence = jnp.where(lane == segments(tile, core, whole), 0.0, MASKED).astype(BF16)
    member = jnp.where(lane == segments(tile, key_core, whole), 1.0, 0.0).astype(BF16)
    here = slice(part * tile, (part + 1) * tile)
    query = jnp.concatenate([query_ref[here, :HEAD_DIM], fence], axis=1)
    groups = []
    for past in range(part + 1):
        span = slice(past * tile, (past + 1) * tile)
        keys = jnp.concatenate([key_ref[span, :HEAD_DIM], member], axis=1)
        scores = scores_of(query, keys)
        if past == part:
            scores = jnp.where(keep, scores, MASKED)
        groups.append(scores)
    return groups


def row_tops(groups):
    joined = functools.reduce(jnp.maximum, groups)
    return jnp.max(joined, axis=-1, keepdims=True)


def weigh(groups, top, value_ref, tile):
    ones = jnp.ones((tile, HEAD_DIM), BF16)
    mixed = None
    for past, scores in enumerate(groups):
        weights = jnp.exp2((scores - top) * EXP2_FACTOR).astype(BF16)
        values = value_ref[past * tile : (past + 1) * tile, HEAD_DIM:]
        term = matmul(weights, jnp.concatenate([values, ones], axis=1))
        mixed = term if mixed is None else mixed + term
    return mixed


def own_side_body(info_ref, mine_ref, mixed_ref, top_ref):
    core = info_ref[0]
    whole = info_ref[1] == 1
    tile = 256
    row = lax.broadcasted_iota(jnp.int32, (tile, tile), 0)
    col = lax.broadcasted_iota(jnp.int32, (tile, tile), 1)
    earlier = col < row
    slot = (row & 15) + 16 * core
    opens = (slot == 0) | (jnp.logical_not(whole) & ((slot == 12) | (slot == 24)))
    alone = (row == col) & opens & (row < 16)
    parts = range(mine_ref.shape[0] // tile)
    scored = [
        side_scores(
            mine_ref, mine_ref, part, tile, core, core, whole,
            (earlier | alone) if part == 0 else earlier,
        )
        for part in parts
    ]
    tops = [row_tops(groups) for groups in scored]
    for part in parts:
        here = slice(part * tile, (part + 1) * tile)
        top = tops[part]
        mixed_ref[here, :] = weigh(scored[part], top, mine_ref, tile)
        top_ref[here, :] = jnp.broadcast_to(top, (tile, HEAD_DIM))


def other_side_body(info_ref, mine_ref, other_ref, mixed_ref, top_ref, out_ref):
    core = info_ref[0]
    whole = info_ref[1] == 1
    tile = 256
    row = lax.broadcasted_iota(jnp.int32, (tile, tile), 0)
    col = lax.broadcasted_iota(jnp.int32, (tile, tile), 1)
    earlier = (col >> 4) < (row >> 4) + core
    parts = range(mine_ref.shape[0] // tile)
    scored = [
        side_scores(mine_ref, other_ref, part, tile, core, 1 - core, whole, earlier)
        for part in parts
    ]
    tops = [row_tops(groups) for groups in scored]
    for part in parts:
        here = slice(part * tile, (part + 1) * tile)
        own_top = top_ref[here, :]
        top = jnp.maximum(jnp.broadcast_to(tops[part], (tile, HEAD_DIM)), own_top)
        shrink = jnp.exp2((own_top - top) * EXP2_FACTOR)
        mixed = weigh(scored[part], jnp.concatenate([top, top], axis=1), other_ref, tile)
        total = mixed[:, HEAD_DIM:] + mixed_ref[here, HEAD_DIM:] * shrink
        sums = mixed[:, :HEAD_DIM] + mixed_ref[here, :HEAD_DIM] * shrink
        out_ref[here, :] = (sums / total).astype(BF16)


def back_body(
    narrow_ref, returned_ref, place_col_ref, weight_ref, own_ref, next_ref, last_ref, far_ref
):
    length = place_col_ref.shape[0]
    parts = []
    for head in range(2):
        spot = lax.broadcasted_iota(jnp.int32, (length, SLOTS), 1)
        pick = (spot == place_col_ref[:, head : head + 1]).astype(F32).astype(BF16)
        parts.append(matmul(pick, returned_ref[head]).astype(BF16))
    attended = jnp.concatenate(parts, axis=1)
    width = own_ref.shape[1]
    groups = weight_ref.shape[1] // width
    for steps, target in ((1, next_ref), (groups - 1, last_ref), (2, far_ref), (0, own_ref)):
        group = lax.rem(narrow_ref[0] + steps, groups)
        columns = pl.ds(pl.multiple_of(group * width, width), width)
        term = matmul(attended, weight_ref[:, columns])
        target[...] = term.astype(target.dtype)


def last_body(
    narrow_ref, own_ref, one_ref, two_ref, three_ref, hidden_ref, out_any, out_ref, sems
):
    length, width = own_ref.shape
    columns = pl.ds(pl.multiple_of(narrow_ref[0] * width, width), width)
    parts = 4
    step = length // parts
    copies = []
    for part in range(parts):
        here = slice(part * step, (part + 1) * step)
        mixed = own_ref[here, :].astype(F32)
        for term_ref in (one_ref, two_ref, three_ref):
            mixed += term_ref[here, :].astype(F32)
        out_ref[here, :] = hidden_ref[here, columns].astype(F32) + mixed
        copy = pltpu.make_async_copy(out_ref.at[here], out_any.at[here], sems.at[part])
        copy.start()
        copies.append(copy)
    for copy in copies:
        copy.wait()


def around(value, steps):
    count = lax.axis_size("narrow")
    return lax.ppermute(value, "narrow", [(i, (i + steps) % count) for i in range(count)])


def around_by_core(value, steps):
    count = lax.axis_size("narrow")
    pairs = [
        (w * count + n, w * count + (n + (steps if w % 2 == 0 else -steps)) % count)
        for w in range(lax.axis_size("wide"))
        for n in range(count)
    ]
    return lax.ppermute(value, ("wide", "narrow"), pairs)


def swap_cores(value):
    count = lax.axis_size("wide")
    return lax.ppermute(value, "wide", [(i, i ^ 1) for i in range(count)])


def shards(tokens, w_qk1, w_value1, w_out1, w_qk2, w_value2, w_out2, cluster_ids):
    length, width = tokens.shape
    shape = jax.ShapeDtypeStruct
    wide = lax.axis_index("wide")
    narrow = lax.axis_index("narrow")
    wide_count = lax.axis_size("wide")
    core = wide & 1
    group_width = w_qk1.shape[1]

    w_first = around_by_core(w_out1, 1)
    w_half = lax.dynamic_slice_in_dim(w_out1, core * HEAD_DIM, HEAD_DIM, 0)

    qk1, value1, tails = call(
        front_body,
        (
            shape((length, group_width), BF16),
            shape((length, group_width), BF16),
            shape((2, WINDOW, group_width), BF16),
        ),
        (tokens, w_qk1, w_value1),
        scratch=(
            pltpu.VMEM((length, width), BF16),
            pltpu.VMEM((width, group_width), BF16),
            pltpu.VMEM((width, group_width), BF16),
            pltpu.SemaphoreType.DMA((4,)),
        ),
        flops=2 * length * width * group_width * 2,
        bytes_accessed=3 * 2**20,
        space=pltpu.HBM,
        mib=53,
    )
    tails, w_half = lax.optimization_barrier((tails, w_half))
    w_far_mine = around(w_half, 2)
    before = lax.ppermute(tails, "wide", [(i, i + 1) for i in range(wide_count - 1)])
    attended1 = call(
        window_body,
        shape((length, group_width), BF16),
        (wide.reshape(1), qk1, value1, before),
        prefetch=1,
        flops=2**20,
        bytes_accessed=2**20,
    )
    attended1, cluster_ids, w_out1_later, w_qk2, w_value2 = lax.optimization_barrier(
        (attended1, cluster_ids, w_out1, w_qk2, w_value2)
    )
    w_second = swap_cores(w_first)
    w_far_other = swap_cores(w_far_mine)
    far = around(attended1, 2)
    first = around_by_core(attended1, 1)
    second = around_by_core(attended1, -1)
    place, place_col, w_out1_near, w_qk2_near, w_value2_near = call(
        place_body,
        (
            shape((2, length), jnp.int32),
            shape((length, 2), jnp.int32),
            shape(w_out1.shape, BF16),
            shape(w_qk2.shape, BF16),
            shape(w_value2.shape, BF16),
        ),
        (cluster_ids, w_out1_later, w_qk2, w_value2),
        scratch=(pltpu.VMEM((2, length), jnp.int32), pltpu.SemaphoreType.DMA((4,))),
        flops=2**33,
        bytes_accessed=2**18,
        space=pltpu.HBM,
    )
    started = call(
        begin_mixed_body,
        shape((length, width), F32),
        (core.reshape(1), tokens, attended1, far, w_out1_near, w_far_mine, w_far_other),
        prefetch=1,
        flops=2**20,
        bytes_accessed=2**22,
    )
    hidden, outgoing = call(
        middle_body,
        (shape((length, width), BF16), shape((2, SLOTS, 2 * HEAD_DIM), BF16)),
        (
            started, first, second, w_first, w_second, w_qk2_near, w_value2_near, place,
        ),
        flops=2**31,
        bytes_accessed=2**23,
    )
    per_pair = 2 * SLOTS // wide_count
    arrived = lax.all_to_all(
        outgoing.reshape(wide_count, per_pair, 2 * HEAD_DIM), "wide", 0, 0, tiled=True
    ).reshape(2 * SLOTS, 2 * HEAD_DIM)
    other = swap_cores(arrived)
    info = jnp.stack([core, (((wide >> 1) & 15) < 8).astype(jnp.int32)])
    rows = 2 * SLOTS
    own_mixed, own_top = call(
        own_side_body,
        (shape((rows, 2 * HEAD_DIM), F32), shape((rows, HEAD_DIM), F32)),
        (info, arrived),
        prefetch=1,
        flops=2**30,
        bytes_accessed=2**21,
    )
    answers = call(
        other_side_body,
        shape((rows, HEAD_DIM), BF16),
        (info, arrived, other, own_mixed, own_top),
        prefetch=1,
        flops=2**30,
        bytes_accessed=2**21,
    )
    returned = lax.all_to_all(
        answers.reshape(wide_count, per_pair, HEAD_DIM), "wide", 0, 0, tiled=True
    ).reshape(2, SLOTS, HEAD_DIM)
    block = shape((length, group_width), BF16)
    own, to_next, to_last, to_far = call(
        back_body,
        (block, block, block, block),
        (narrow.reshape(1), returned, place_col, w_out2),
        prefetch=1,
        flops=2**29,
        bytes_accessed=2**21,
    )
    return call(
        last_body,
        shape((length, group_width), F32),
        (
            narrow.reshape(1), own, around(to_far, 2), around(to_next, 1),
            around(to_last, -1), hidden,
        ),
        scratch=(
            pltpu.VMEM((length, group_width), F32),
            pltpu.SemaphoreType.DMA((4,)),
        ),
        out_space=pl.ANY,
        prefetch=1,
        flops=2**22,
        bytes_accessed=2**21,
    )


def solution(mesh):
    placed = (
        P("wide", None),
        P(None, "narrow"),
        P(None, "narrow"),
        P("narrow", None),
        P(None, "narrow"),
        P(None, "narrow"),
        P("narrow", None),
        P("narrow", "wide"),
    )
    return jax.shard_map(
        shards, mesh=mesh, in_specs=placed, out_specs=P("wide", "narrow"), check_vma=False
    )
```
